256 devices in a mesh: seq: 64 (over y, x_lo, z), head: 4 (over x_hi, core).
Axes of the slice: x: 4 (x_hi: 2, x_lo: 2; x = x_hi * 2 + x_lo), y: 4, z: 8, core: 2. Of those that a mesh axis runs over, the one named last changes fastest.
Arguments:
- queries: bfloat16 [16384, 32, 128], P('seq', 'head'), may hold values from -6 to 6, as said below
- key_states: bfloat16 [16384, 4, 128], P('seq', 'head'), may hold values from -6 to 6, as said below
- value_vectors_all: bfloat16 [16384, 4, 128], P('seq', 'head'), may hold values from -6 to 6
- out_weight: bfloat16 [4096, 4096], P('head'), may hold values from -0.125 to 0.125
Outputs:
- mixed: bfloat16 [16384, 4096], P('seq', 'head')
The draws below stay inside these ranges and needn't reach their ends.
Inputs may be any that keep to these rules, and one draw needn't show every extreme that they name: `queries`: query vectors; entries of order one. `key_states`: key vectors; entries of order one.
All inputs are finite; a program needn't handle non-finite values.
Results may differ from the reference program's by a relative error of at most 0.015.
Values may be sent and summed in bfloat16 or wider, within the bound.
No kernel may reach another device: no remote copies, remote signals or barrier semaphores. Data moves between devices by JAX's collectives and lax.ppermute only.
A program may use at most 64 MiB of HBM per device.

```python
import math
import jax
import jax.numpy as jnp
from jax import lax

QUERY_HEADS = 32
KEY_VALUE_HEADS = 4
HEAD_SIZE = 128
D = 4096
TOK_DEV = 256
SEQUENCE_TOKENS = 16384


def shared_normal(key):
    return jax.random.normal(key, (SEQUENCE_TOKENS, KEY_VALUE_HEADS, HEAD_SIZE), jnp.float32)


def draw_key_states(key, part):
    shared = shared_normal(key)
    return jnp.clip(1.7 * shared, -6.0, 6.0).astype(jnp.bfloat16)


def draw_queries(key, part):
    key = jax.random.fold_in(key, 23)
    own_field = jax.random.normal(key, (SEQUENCE_TOKENS, QUERY_HEADS, HEAD_SIZE), jnp.float32)
    return jnp.clip(1.7 * own_field, -6.0, 6.0).astype(jnp.bfloat16)


def strengthened(array, own_key, source, target, blocks, factor):
    owner, partner = [(jnp.arange(array.shape[dim]) // (array.shape[dim] // blocks)).reshape([-1 if axis == dim else 1 for axis in range(array.ndim)]) for dim in (source, target)]
    chosen = jax.random.permutation(own_key, blocks)[partner]
    strong = (owner == chosen) | (owner == (partner + blocks // 2) % blocks)
    return jnp.where(strong, factor * array, array)


def block_scale(key, shape, cuts, low, largest):
    loudness = 1.0
    for position, blocks in cuts:
        draws = jax.random.uniform(jax.random.fold_in(jax.random.fold_in(key, 6), position), (blocks,), jnp.float32, low / len(cuts), largest / len(cuts))
        loudness = loudness * jnp.repeat(jnp.exp(draws), shape[position] // blocks).reshape((-1,) + (1,) * (len(shape) - 1 - position))
    return loudness


def noise(own_key, extent, width, reach, pieces=(), kind=jnp.bfloat16):
    values = jax.random.normal(own_key, extent, jnp.float32) * width
    if len(pieces) > 0:
        values = block_scale(own_key, extent, pieces, -0.22, 0.18) * values
    return jnp.clip(values, min=-reach, max=reach).astype(kind)


def gaussian_with(own_key, shape, deviation, limit, split, heavy, kind=jnp.bfloat16):
    array = deviation * jax.random.normal(own_key, shape, jnp.float32)
    if split:
        array = array * block_scale(own_key, shape, split, -0.22, 0.18)
    return jnp.clip(strengthened(array, jax.random.fold_in(own_key, 3), *heavy), -limit, limit).astype(kind)


def setup_inputs(seed: int = 0) -> dict:
    keys = jax.random.split(jax.random.key(seed), 5)
    return {
        "queries": draw_queries(jax.random.fold_in(keys[4], 71), 0),
        "key_states": draw_key_states(jax.random.fold_in(keys[4], 71), 0),
        "value_vectors_all": noise(keys[2], (SEQUENCE_TOKENS, KEY_VALUE_HEADS, HEAD_SIZE), 1.0, 6.0, ((0, 64), (1, 4))),
        "out_weight": gaussian_with(keys[3], (QUERY_HEADS * HEAD_SIZE, D), (QUERY_HEADS * HEAD_SIZE) ** -0.5, 0.125, ((0, 4),), (0, 1, 4, 2.0)),
    }


def attend_block(query_tile_block, query_start, key_full, value_full):
    token_count = query_tile_block.shape[0]
    group_width = QUERY_HEADS // KEY_VALUE_HEADS
    query_portion = query_tile_block.astype(jnp.float32).reshape(token_count, KEY_VALUE_HEADS, group_width, HEAD_SIZE)
    scores = jnp.einsum('tkgd,skd->kgts', query_portion, key_full) * (1.0 / math.sqrt(HEAD_SIZE))
    query_pos = query_start + jnp.arange(token_count, dtype=jnp.int32)
    key_pos = jnp.arange(SEQUENCE_TOKENS, dtype=jnp.int32)
    allowed = key_pos[None, :] <= query_pos[:, None]
    scores = jnp.where(allowed, scores, -1e+30)
    running_max = lax.optimization_barrier(jnp.max(scores, axis=-1, keepdims=True))
    weights = jnp.where(allowed, jnp.exp(scores - running_max), 0.0)
    running_sum = lax.optimization_barrier(jnp.sum(weights, axis=-1))
    probs = weights.astype(jnp.bfloat16).astype(jnp.float32)
    numerator = jnp.einsum('kgts,skd->kgtd', probs, value_full)
    result = numerator / running_sum[..., None]
    return result.transpose(2, 0, 1, 3).reshape(token_count, QUERY_HEADS, HEAD_SIZE).astype(jnp.bfloat16)

def reference(queries, key_states, value_vectors_all, out_weight):
    block_count = SEQUENCE_TOKENS // TOK_DEV
    key_full = key_states.astype(jnp.float32)
    value_full = value_vectors_all.astype(jnp.float32)
    blocks = queries.reshape(block_count, TOK_DEV, QUERY_HEADS, HEAD_SIZE)
    starts = jnp.arange(block_count, dtype=jnp.int32) * TOK_DEV

    def one_block(pair):
        return attend_block(pair[0], pair[1], key_full, value_full)
    attended = lax.map(one_block, (blocks, starts)).reshape(SEQUENCE_TOKENS, QUERY_HEADS * HEAD_SIZE)
    return jnp.dot(attended, out_weight, preferred_element_type=jnp.float32).astype(jnp.bfloat16)
```

```python
import functools
import math

import jax
import jax.numpy as jnp
from jax import lax
from jax.experimental import pallas as pl
from jax.experimental.pallas import tpu as pltpu
from jax.sharding import PartitionSpec as P

NY, NX, NZ = 4, 2, 8
TOK = 256
HALF = 128
HEADS = 8
HD = 128
ROWS = TOK * HEADS
SLOTS = NY * NZ
KEYS = SLOTS * TOK
KT = 1024
RC = 256
SCALE2 = math.log2(math.e) / math.sqrt(HD)
LOW, HIGH = 1e-20, 1e34
NEG = -1e30
AXES = ("seq", "head")
BOTH = (((1,), (1,)), ((), ()))


def device(X, y, x, z, c):
    return ((y % NY) * 16 + x * 8 + z % NZ) * 4 + X * 2 + c


def perm_of(f):
    return [
        (device(X, y, x, z, c), device(*f(X, y, x, z, c)))
        for y in range(NY)
        for x in range(NX)
        for z in range(NZ)
        for X in range(2)
        for c in range(2)
    ]


def sign_of(pos, c):
    return 1 - 2 * ((pos + c) % 2)


SWAP = perm_of(lambda X, y, x, z, c: (X, y, x, z, c) if c == x else (X, 3 - y, 1 - x, z, 1 - c))
CORE = perm_of(lambda X, y, x, z, c: (X, y, x, z, 1 - c))
XHI = perm_of(lambda X, y, x, z, c: (1 - X, y, x, z, c))
Z_NEAR = perm_of(lambda X, y, x, z, c: (X, y, x, z + sign_of(z, c), c))
Z_FAR = perm_of(lambda X, y, x, z, c: (X, y, x, z - sign_of(z, c), c))
Y_NEAR = perm_of(lambda X, y, x, z, c: (X, y + sign_of(y, c), x, z, c))
Y_FAR = perm_of(lambda X, y, x, z, c: (X, y - sign_of(y, c), x, z, c))


def send(value, perm):
    return lax.ppermute(value, AXES, perm)


def ring_z(own, z, s):
    r1 = send(own, Z_NEAR)
    first = jnp.concatenate([own, r1], axis=0)
    r2 = send(first, Z_FAR)
    r3 = send(r2, Z_NEAR)
    r4 = send(r3, Z_FAR)
    where = [(z, z + s), (z - s, z - 2 * s), (z + 2 * s, z + 3 * s), (z - 3 * s, z - 4 * s)]
    return [first, r2, r3, r4], [[w % NZ for w in pair] for pair in where]


def ring_y(own, y, s):
    r1 = send(own, Y_NEAR)
    first = jnp.concatenate([own, r1], axis=0)
    r2 = send(first, Y_FAR)
    return [first, r2], [[y, (y + s) % NY], [(y - s) % NY, (y - 2 * s) % NY]]


def mask_tile(s, start, limit):
    key = start + lax.broadcasted_iota(jnp.int32, s.shape, 1)
    tok = lax.broadcasted_iota(jnp.int32, s.shape, 0)
    return jnp.where(key <= limit + tok, s, NEG)


def score(q, k):
    return lax.dot_general(q, k, BOTH, preferred_element_type=jnp.float32) * SCALE2


def fast_tile(q_ref, k_ref, v_ref, acc, t, slot, masked):
    start = pl.multiple_of(t * KT, KT)
    k = k_ref[pl.ds(start, KT), :]
    v = v_ref[pl.ds(start, KT), :]
    for r in range(ROWS // RC):
        rs = pl.ds(r * RC, RC)
        s = score(q_ref[rs, :], k)
        if masked:
            s = mask_tile(s, start, slot * TOK)
        p = jnp.exp2(s).astype(jnp.bfloat16)
        acc[rs, :] += jnp.dot(p, v, preferred_element_type=jnp.float32)


def slow_tile(q_ref, k_ref, v_ref, acc, top, t, limit, causal):
    start = pl.multiple_of(t * KT, KT)

    def chunk(r, _):
        rs = pl.ds(pl.multiple_of(r * RC, RC), RC)
        k = k_ref[pl.ds(start, KT), :]
        s = score(q_ref[rs, :], k)
        if causal:
            s = mask_tile(s, start, limit)
        old = top[rs, :]
        new = jnp.maximum(old, jnp.max(s, axis=1, keepdims=True))
        p = jnp.exp2(s - new[:, :1]).astype(jnp.bfloat16)
        shrink = jnp.exp2(old - new)[:, :1]
        acc[rs, :] = acc[rs, :] * shrink + jnp.dot(
            p, v_ref[pl.ds(start, KT), :], preferred_element_type=jnp.float32
        )
        top[rs, :] = new
        return 0

    lax.fori_loop(0, ROWS // RC, chunk, 0)


def eye():
    a = lax.broadcasted_iota(jnp.int32, (128, 128), 0)
    b = lax.broadcasted_iota(jnp.int32, (128, 128), 1)
    return a == b


def attend(q_ref, k_ref, v_ref, acc, top, out_ref, n_full, slot, causal):
    acc[...] = jnp.zeros_like(acc)
    top[...] = jnp.zeros_like(top)

    def step(t, _):
        fast_tile(q_ref, k_ref, v_ref, acc, t, slot, False)
        return 0

    lax.fori_loop(0, n_full, step, 0)
    if causal:
        fast_tile(q_ref, k_ref, v_ref, acc, n_full, slot, True)
    total = acc[:, HD:]
    bad = jnp.logical_not(jnp.logical_and(total >= LOW, total <= HIGH))
    n_bad = jnp.sum(jnp.max(bad.astype(jnp.float32), axis=0, keepdims=True))
    some = n_full >= 0 if causal else n_full > 0

    @pl.when(jnp.logical_not(some))
    def _():
        top[...] = jnp.full_like(top, NEG)

    @pl.when(jnp.logical_and(some, n_bad > 0.0))
    def _():
        acc[...] = jnp.zeros_like(acc)
        top[...] = jnp.full_like(top, NEG)

        def again(t, _):
            slow_tile(q_ref, k_ref, v_ref, acc, top, t, 0, False)
            return 0

        lax.fori_loop(0, n_full, again, 0)
        if causal:
            slow_tile(q_ref, k_ref, v_ref, acc, top, n_full, slot * TOK, True)

    out_ref[:ROWS, :] = acc[:, :HD]
    diagonal = eye()
    for i in range(ROWS // 128):
        rs = pl.ds(i * 128, 128)
        row = jnp.sum(jnp.where(diagonal, acc[rs, HD:], 0.0), axis=0, keepdims=True)
        out_ref[ROWS + i : ROWS + i + 1, :] = row
        row = jnp.sum(jnp.where(diagonal, top[rs, :], 0.0), axis=0, keepdims=True)
        out_ref[ROWS + 16 + i : ROWS + 17 + i, :] = row


def attention_kernel(n_pieces, info, places, *refs):
    q_own, q_other = refs[0], refs[1]
    pieces = refs[2 : 2 + n_pieces]
    keep_ref, give_ref = refs[2 + n_pieces], refs[3 + n_pieces]
    k_ref, v_ref, acc, top = refs[4 + n_pieces :]
    v_ref[:, HD:] = jnp.ones((KEYS, HD), jnp.bfloat16)
    base = 0
    for piece in pieces:
        count = piece.shape[0] // TOK

        def place(i, _, piece=piece, base=base):
            src = pl.multiple_of(i * TOK, TOK)
            dst = pl.multiple_of(places[base + i], HALF)
            k_ref[pl.ds(dst, HALF), :] = piece[pl.ds(src, HALF), :]
            v_ref[pl.ds(dst, HALF), :HD] = piece[pl.ds(src + HALF, HALF), :]
            return 0

        lax.fori_loop(0, count, place, 0)
        base += count
    attend(q_other, k_ref, v_ref, acc, top, give_ref, info[1], 0, False)
    attend(q_own, k_ref, v_ref, acc, top, keep_ref, info[0] // (KT // TOK), info[0], True)


def attention(info, places, q_own, q_other, pieces):
    vmem = pl.BlockSpec(memory_space=pltpu.VMEM)
    smem = pl.BlockSpec(memory_space=pltpu.SMEM)
    part = jax.ShapeDtypeStruct((ROWS + 32, HD), jnp.float32)
    return pl.pallas_call(
        functools.partial(attention_kernel, len(pieces)),
        out_shape=(part, part),
        in_specs=[smem, smem] + [vmem] * (2 + len(pieces)),
        out_specs=(vmem, vmem),
        scratch_shapes=[
            pltpu.VMEM((KEYS, HD), jnp.bfloat16),
            pltpu.VMEM((KEYS, 2 * HD), jnp.bfloat16),
            pltpu.VMEM((ROWS, 2 * HD), jnp.float32),
            pltpu.VMEM((ROWS, HD), jnp.float32),
        ],
        compiler_params=pltpu.CompilerParams(vmem_limit_bytes=40 * 2**20),
        name="attention",
    )(info, places, q_own, q_other, *pieces)


def merge_kernel(a_ref, b_ref, out_ref):
    diagonal = eye()

    def column(ref, row):
        wide = jnp.where(diagonal, ref[row : row + 1, :], 0.0)
        return jnp.sum(wide, axis=1, keepdims=True)

    for i in range(ROWS // 128):
        rs = pl.ds(i * 128, 128)
        top_a, top_b = column(a_ref, ROWS + 16 + i), column(b_ref, ROWS + 16 + i)
        top = jnp.maximum(top_a, top_b)
        fa, fb = jnp.exp2(top_a - top), jnp.exp2(top_b - top)
        total = column(a_ref, ROWS + i) * fa + column(b_ref, ROWS + i) * fb
        value = (a_ref[rs, :] * fa + b_ref[rs, :] * fb) / total
        head, tok = divmod(i * 128, TOK)
        out_ref[tok : tok + 128, head * HD : (head + 1) * HD] = value.astype(jnp.bfloat16)


def merge(a, b):
    vmem = pl.BlockSpec(memory_space=pltpu.VMEM)
    return pl.pallas_call(
        merge_kernel,
        out_shape=jax.ShapeDtypeStruct((TOK, HEADS * HD), jnp.bfloat16),
        in_specs=[vmem, vmem],
        out_specs=vmem,
        name="merge",
    )(a, b)


COLS = 512


def project_kernel(first, x_ref, w_ref, give_ref, keep_ref):
    value = jnp.dot(x_ref[...], w_ref[...], preferred_element_type=jnp.float32)
    i = pl.program_id(0)

    @pl.when(i < 2)
    def _():
        give_ref[...] = value.astype(jnp.bfloat16)

    @pl.when(i >= 2)
    def _():
        keep_ref[...] = value


def project(x, w, give, keep):
    first = jnp.stack([give, keep]).astype(jnp.int32) * 2
    depth = x.shape[1]
    grid_spec = pltpu.PrefetchScalarGridSpec(
        num_scalar_prefetch=1,
        grid=(4,),
        in_specs=[
            pl.BlockSpec((TOK, depth), lambda i, f: (0, 0)),
            pl.BlockSpec((depth, COLS), lambda i, f: (0, f[i // 2] + i % 2)),
        ],
        out_specs=[
            pl.BlockSpec((TOK, COLS), lambda i, f: (0, jnp.minimum(i, 1))),
            pl.BlockSpec((TOK, COLS), lambda i, f: (0, jnp.maximum(i - 2, 0))),
        ],
    )
    return pl.pallas_call(
        project_kernel,
        grid_spec=grid_spec,
        out_shape=(
            jax.ShapeDtypeStruct((TOK, 1024), jnp.bfloat16),
            jax.ShapeDtypeStruct((TOK, 1024), jnp.float32),
        ),
        compiler_params=pltpu.CompilerParams(vmem_limit_bytes=24 * 2**20),
        name="project",
    )(first, x, w)


def on_device(queries, key_states, value_vectors_all, out_weight):
    seq = lax.axis_index("seq")
    head = lax.axis_index("head")
    y, x, z = seq // 16, (seq // 8) % 2, seq % 8
    X, c = head // 2, head % 2
    diagonal = c == x

    k = key_states.reshape(2, 1, HALF, HD)
    v = value_vectors_all.reshape(2, 1, HALF, HD)
    kv = send(jnp.concatenate([k, v], axis=1).reshape(2 * TOK, HD), SWAP)
    q = queries.transpose(1, 0, 2).reshape(ROWS, HD)
    q_own = send(q, SWAP)
    q_other = send(q_own, CORE)

    sz, sy = sign_of(z, c), sign_of(y, c)
    za, wa = ring_z(kv[:TOK], z, sz)
    plane = jnp.concatenate(za, axis=0)
    za_z = [w for pair in wa for w in pair]
    ya, ya_y = ring_y(plane, y, sy)
    yb, yb_y = ring_y(kv[TOK:], y, sy)
    column = jnp.concatenate(yb, axis=0)
    yb_all = [w for pair in yb_y for w in pair]
    zb, zb_z = ring_z(column, z, sz)

    def block_row(chip_y):
        return jnp.where(diagonal, chip_y, NY - 1 - chip_y)

    def place(chip_y, chip_z, half):
        return (block_row(chip_y) * NZ + chip_z) * TOK + half * HALF

    places = [place(wy, wz, 0) for pair in ya_y for wy in pair for wz in za_z]
    places += [place(wy, wz, 1) for pair in zb_z for wz in pair for wy in yb_all]
    own_row = block_row(y)
    own_slot = own_row * NZ + z
    other_tiles = ((NY - 1 - own_row) + jnp.where(c == 0, 1, 0)) * (NZ * TOK // KT)
    info = jnp.stack([own_slot, other_tiles]).astype(jnp.int32)
    keep, give = attention(info, jnp.stack(places).astype(jnp.int32), q_own, q_other, ya + zb)
    attended = send(merge(keep, send(give, CORE)), SWAP)

    far_give, far_keep = project(attended, out_weight, (1 - X) * 2 + 1 - c, (1 - X) * 2 + c)
    far = far_keep + send(far_give, CORE).astype(jnp.float32)
    far = send(far.astype(jnp.bfloat16), XHI)
    near_give, near_keep = project(attended, out_weight, X * 2 + 1 - c, X * 2 + c)
    near = near_keep + send(near_give, CORE).astype(jnp.float32)
    return (near + far.astype(jnp.float32)).astype(jnp.bfloat16)


def solution(mesh):
    in_specs = (
        P("seq", "head", None),
        P("seq", "head", None),
        P("seq", "head", None),
        P("head", None),
    )
    out_specs = P("seq", "head")
    return jax.shard_map(
        on_device, mesh=mesh, in_specs=in_specs, out_specs=out_specs, check_vma=False
    )
```

```python
import functools
import math

import jax
import jax.numpy as jnp
from jax import lax
from jax.experimental import pallas as pl
from jax.experimental.pallas import tpu as pltpu
from jax.sharding import PartitionSpec as P

NY, NX, NZ = 4, 2, 8
TOK = 256
HEADS = 8
HD = 128
ROWS = TOK * HEADS
SLOTS = NY * NZ
KEYS = SLOTS * TOK
KT = 1024
RC = 256
PER_TILE = KT // TOK
SCALE2 = math.log2(math.e) / math.sqrt(HD)
LOW, HIGH = 1e-20, 1e34
NEG = -1e30
AXES = ("seq", "head")
BOTH = (((1,), (1,)), ((), ()))


def device(X, y, x, z, c):
    return ((y % NY) * 16 + x * 8 + z % NZ) * 4 + X * 2 + c


def perm_of(f):
    return [
        (device(X, y, x, z, c), device(*f(X, y, x, z, c)))
        for y in range(NY)
        for x in range(NX)
        for z in range(NZ)
        for X in range(2)
        for c in range(2)
    ]


def sign_of(pos, c):
    return 1 - 2 * ((pos + c) % 2)


SWAP = perm_of(lambda X, y, x, z, c: (X, y, x, z, c) if c == x else (X, 3 - y, 1 - x, z, 1 - c))
SWAP_BACK = [pair for pair in SWAP if pair[0] != pair[1]]
CORE = perm_of(lambda X, y, x, z, c: (X, y, x, z, 1 - c))
XHI = perm_of(lambda X, y, x, z, c: (1 - X, y, x, z, c))
Z_NEAR = perm_of(lambda X, y, x, z, c: (X, y, x, z + sign_of(z, c), c))
Z_FAR = perm_of(lambda X, y, x, z, c: (X, y, x, z - sign_of(z, c), c))
Y_NEAR = perm_of(lambda X, y, x, z, c: (X, y + sign_of(y, c), x, z, c))
Y_FAR = perm_of(lambda X, y, x, z, c: (X, y - sign_of(y, c), x, z, c))


def send(value, perm):
    return lax.ppermute(value, AXES, perm)


def score(q, k):
    return lax.dot_general(q, k, BOTH, preferred_element_type=jnp.float32) * SCALE2


def mask_tile(s, zs, first, z):
    key = lax.broadcasted_iota(jnp.int32, (RC, TOK), 1)
    tok = lax.broadcasted_iota(jnp.int32, (RC, TOK), 0)
    parts = []
    for i in range(PER_TILE):
        ahead = (z - zs[first + i]) * TOK
        parts.append(jnp.where(key <= tok + ahead, s[:, i * TOK : (i + 1) * TOK], NEG))
    return jnp.concatenate(parts, axis=1)


def fast_tile(q_ref, k_ref, v_ref, acc, q0, k0, mask):
    k = k_ref[pl.ds(k0, KT), :]
    v = v_ref[pl.ds(k0, KT), :]
    for r in range(ROWS // RC):
        rs = pl.ds(pl.multiple_of(q0 + r * RC, RC), RC)
        s = score(q_ref[rs, :], k)
        if mask is not None:
            s = mask(s)
        p = jnp.exp2(s).astype(jnp.bfloat16)
        acc[rs, :] += jnp.dot(p, v, preferred_element_type=jnp.float32)


def slow_tile(q_ref, k_ref, v_ref, acc, top, q0, k0, mask):
    def chunk(r, _):
        rs = pl.ds(pl.multiple_of(q0 + r * RC, RC), RC)
        s = score(q_ref[rs, :], k_ref[pl.ds(k0, KT), :])
        if mask is not None:
            s = mask(s)
        old = top[rs, :]
        new = jnp.maximum(old, jnp.max(s, axis=1, keepdims=True))
        p = jnp.exp2(s - new[:, :1]).astype(jnp.bfloat16)
        shrink = jnp.exp2(old - new)[:, :1]
        acc[rs, :] = acc[rs, :] * shrink + jnp.dot(
            p, v_ref[pl.ds(k0, KT), :], preferred_element_type=jnp.float32
        )
        top[rs, :] = new
        return 0

    lax.fori_loop(0, ROWS // RC, chunk, 0)


def tiles(run, info, rows, zs, first, n_tiles, k_base, block):
    q0 = pl.multiple_of(block * ROWS, ROWS)

    def step(t, _):
        k0 = pl.multiple_of(k_base + t * KT, KT)
        at = (first + t) * PER_TILE
        row = rows[first + t]
        nearest = zs[at]
        for i in range(1, PER_TILE):
            nearest = jnp.minimum(nearest, zs[at + i])

        @pl.when(row < info[block])
        def _():
            run(q0, k0, None)

        @pl.when(jnp.logical_and(row == info[2 + block], nearest <= info[4]))
        def _():
            run(q0, k0, lambda s: mask_tile(s, zs, at, info[4]))

        return 0

    lax.fori_loop(0, n_tiles, step, 0)


def place(piece, k_ref, v_ref, k0):
    for i in range(PER_TILE):
        src, dst = 2 * i * TOK, k0 + i * TOK
        k_ref[dst : dst + TOK, :] = piece[src : src + TOK, :]
        v_ref[dst : dst + TOK, :HD] = piece[src + TOK : src + 2 * TOK, :]


def fast_blocks(info, rows, zs, first, n_tiles, k_base, q_ref, k_ref, v_ref, acc):
    def run(q0, k0, mask):
        fast_tile(q_ref, k_ref, v_ref, acc, q0, k0, mask)

    def block_step(block, _):
        tiles(run, info, rows, zs, first, n_tiles, k_base, block)
        return 0

    lax.fori_loop(0, 2, block_step, 0)


def piece_kernel(first, n_tiles, has_state, info, rows, zs, q_ref, *refs):
    pieces, refs = refs[:n_tiles], refs[n_tiles:]
    acc, k_ref, v_ref = refs[-3:]
    if not has_state:
        acc[...] = jnp.zeros_like(acc)
    v_ref[:, HD:] = jnp.ones((n_tiles * KT, HD), jnp.bfloat16)
    for t, piece in enumerate(pieces):
        place(piece, k_ref, v_ref, t * KT)
    fast_blocks(info, rows, zs, first, n_tiles, 0, q_ref, k_ref, v_ref, acc)


VMEM = pl.BlockSpec(memory_space=pltpu.VMEM)
SMEM = pl.BlockSpec(memory_space=pltpu.SMEM)
STATE = jax.ShapeDtypeStruct((2 * ROWS, 2 * HD), jnp.float32)


def cost(n_tiles):
    return pl.CostEstimate(
        flops=8 * n_tiles * ROWS * KT * HD,
        bytes_accessed=4 * 2**20,
        transcendentals=n_tiles * ROWS * KT,
    )


def attend_pieces(info, rows, zs, q, pieces, first, state=None):
    n_tiles = len(pieces)
    extra = [] if state is None else [state]
    return pl.pallas_call(
        functools.partial(piece_kernel, first, n_tiles, state is not None),
        out_shape=STATE,
        in_specs=[SMEM, SMEM, SMEM, VMEM] + [VMEM] * (n_tiles + len(extra)),
        out_specs=VMEM,
        scratch_shapes=[
            pltpu.VMEM((n_tiles * KT, HD), jnp.bfloat16),
            pltpu.VMEM((n_tiles * KT, 2 * HD), jnp.bfloat16),
        ],
        compiler_params=pltpu.CompilerParams(vmem_limit_bytes=16 * 2**20),
        input_output_aliases={} if state is None else {4 + n_tiles: 0},
        cost_estimate=cost(n_tiles),
        name=f"attend_{first}",
    )(info, rows, zs, q, *pieces, *extra)


def eye():
    a = lax.broadcasted_iota(jnp.int32, (128, 128), 0)
    b = lax.broadcasted_iota(jnp.int32, (128, 128), 1)
    return a == b


def last_kernel(n_pieces, info, rows, zs, q_ref, state, *refs):
    pieces = refs[:n_pieces]
    acc, keep_ref, give_ref, k_ref, v_ref, top = refs[n_pieces:]
    last = n_pieces - 1
    v_ref[last * KT :, HD:] = jnp.ones((KT, HD), jnp.bfloat16)
    place(pieces[last], k_ref, v_ref, last * KT)
    fast_blocks(info, rows, zs, last, 1, last * KT, q_ref, k_ref, v_ref, acc)
    diagonal = eye()

    def transpose_rows(ref, lanes, q0, out_ref, at):
        for i in range(ROWS // 128):
            rs = pl.ds(q0 + i * 128, 128)
            row = jnp.sum(jnp.where(diagonal, ref[rs, lanes], 0.0), axis=0, keepdims=True)
            out_ref[at + i : at + i + 1, :] = row

    for block, out_ref in enumerate((keep_ref, give_ref)):
        q0 = block * ROWS
        mine = pl.ds(q0, ROWS)
        total = acc[mine, HD:]
        bad = jnp.logical_not(jnp.logical_and(total >= LOW, total <= HIGH))
        n_bad = jnp.sum(jnp.max(bad.astype(jnp.float32), axis=0, keepdims=True))
        some = jnp.logical_or(info[block] > 0, info[2 + block] >= 0)
        out_ref[ROWS + 16 :, :] = jnp.full((16, HD), jnp.where(some, 0.0, NEG), jnp.float32)

        @pl.when(jnp.logical_and(some, n_bad > 0.0))
        def _(mine=mine, block=block, q0=q0, out_ref=out_ref):
            acc[mine, :] = jnp.zeros((ROWS, 2 * HD), jnp.float32)
            top[mine, :] = jnp.full((ROWS, HD), NEG, jnp.float32)
            v_ref[: last * KT, HD:] = jnp.ones((last * KT, HD), jnp.bfloat16)
            for t, piece in enumerate(pieces[:last]):
                place(piece, k_ref, v_ref, t * KT)

            def run(q0, k0, mask):
                slow_tile(q_ref, k_ref, v_ref, acc, top, q0, k0, mask)

            tiles(run, info, rows, zs, 0, n_pieces, 0, block)
            transpose_rows(top, slice(None), q0, out_ref, ROWS + 16)

        out_ref[:ROWS, :] = acc[mine, :HD]
        transpose_rows(acc, slice(HD, 2 * HD), q0, out_ref, ROWS)


def attend_last(info, rows, zs, q, state, pieces):
    part = jax.ShapeDtypeStruct((ROWS + 32, HD), jnp.float32)
    return pl.pallas_call(
        functools.partial(last_kernel, len(pieces)),
        out_shape=(STATE, part, part),
        in_specs=[SMEM, SMEM, SMEM] + [VMEM] * (2 + len(pieces)),
        out_specs=(VMEM, VMEM, VMEM),
        scratch_shapes=[
            pltpu.VMEM((KEYS, HD), jnp.bfloat16),
            pltpu.VMEM((KEYS, 2 * HD), jnp.bfloat16),
            pltpu.VMEM((2 * ROWS, HD), jnp.float32),
        ],
        input_output_aliases={4: 0},
        compiler_params=pltpu.CompilerParams(vmem_limit_bytes=20 * 2**20),
        cost_estimate=cost(1),
        name="attend_last",
    )(info, rows, zs, q, state, *pieces)[1:]


def merge_kernel(a_ref, b_ref, out_ref):
    n = ROWS // 128
    sums, tops = pl.ds(ROWS, n), pl.ds(ROWS + n, n)
    top = jnp.maximum(a_ref[tops, :], b_ref[tops, :])
    fa, fb = jnp.exp2(a_ref[tops, :] - top), jnp.exp2(b_ref[tops, :] - top)
    total = a_ref[sums, :] * fa + b_ref[sums, :] * fb
    share = jnp.concatenate([fa / total, fb / total, jnp.zeros((128 - 2 * n, 128), jnp.float32)], axis=0)
    share = share.T
    for i in range(n):
        rs = pl.ds(i * 128, 128)
        value = a_ref[rs, :] * share[:, i : i + 1] + b_ref[rs, :] * share[:, n + i : n + i + 1]
        head, tok = divmod(i * 128, TOK)
        out_ref[tok : tok + 128, head * HD : (head + 1) * HD] = value.astype(jnp.bfloat16)


def merge(a, b):
    return pl.pallas_call(
        merge_kernel,
        out_shape=jax.ShapeDtypeStruct((TOK, HEADS * HD), jnp.bfloat16),
        in_specs=[VMEM, VMEM],
        out_specs=VMEM,
        compiler_params=pltpu.CompilerParams(vmem_limit_bytes=8 * 2**20),
        name="merge",
    )(a, b)


COLS = 512
SLICE = 1024


def load_kernel(first, info, w_ref, out_ref, sem):
    col = pl.multiple_of(info[first] * SLICE, SLICE)
    copy = pltpu.make_async_copy(w_ref.at[:, pl.ds(col, 2 * SLICE)], out_ref, sem)
    copy.start()
    copy.wait()


def load_columns(info, w, first):
    return pl.pallas_call(
        functools.partial(load_kernel, first),
        out_shape=jax.ShapeDtypeStruct((w.shape[0], 2 * SLICE), w.dtype),
        in_specs=[SMEM, pl.BlockSpec(memory_space=pltpu.HBM)],
        out_specs=VMEM,
        scratch_shapes=[pltpu.SemaphoreType.DMA],
        compiler_params=pltpu.CompilerParams(vmem_limit_bytes=4 * 2**20),
        cost_estimate=pl.CostEstimate(flops=0, bytes_accessed=2**23, transcendentals=0),
        name=f"load_{first}",
    )(info, w)


def project_kernel(info, home_ref, away_ref, w_ref, give_ref, keep_ref, x_ref):
    x_ref[...] = home_ref[...]

    @pl.when(info[5] == 0)
    def _():
        x_ref[...] = away_ref[...]

    for out_ref, side in ((give_ref, 1 - info[6]), (keep_ref, info[6])):
        for j in range(0, SLICE, COLS):
            at = pl.ds(pl.multiple_of(side * SLICE + j, COLS), COLS)
            value = jnp.dot(x_ref[...], w_ref[:, at], preferred_element_type=jnp.float32)
            out_ref[:, j : j + COLS] = value.astype(out_ref.dtype)


def project(info, home, away, w):
    return pl.pallas_call(
        project_kernel,
        out_shape=(
            jax.ShapeDtypeStruct((TOK, SLICE), jnp.bfloat16),
            jax.ShapeDtypeStruct((TOK, SLICE), jnp.float32),
        ),
        in_specs=[SMEM, VMEM, VMEM, VMEM],
        out_specs=(VMEM, VMEM),
        scratch_shapes=[pltpu.VMEM((TOK, SLICE), jnp.bfloat16)],
        compiler_params=pltpu.CompilerParams(vmem_limit_bytes=8 * 2**20),
        name="project",
    )(info, home, away, w)


def on_device(queries, key_states, value_vectors_all, out_weight):
    seq = lax.axis_index("seq")
    head = lax.axis_index("head")
    y, x, z = seq // 16, (seq // 8) % 2, seq % 8
    X, c = head // 2, head % 2
    diagonal = c == x

    k = key_states.reshape(TOK, HD)
    v = value_vectors_all.reshape(TOK, HD)
    kv = send(jnp.concatenate([k, v], axis=0), SWAP)
    kv, queries = lax.optimization_barrier((kv, queries))
    q = queries.transpose(1, 0, 2).reshape(ROWS, HD)
    q_own = send(q, SWAP)
    q_other = send(q_own, CORE)

    sz, sy = sign_of(z, c), sign_of(y, c)
    near_z = send(kv, Z_NEAR)
    pair = jnp.concatenate([kv, near_z], axis=0)
    far_z = send(pair, Z_FAR)
    a = jnp.concatenate([pair, far_z], axis=0)
    far_z, q_own = lax.optimization_barrier((far_z, q_own))
    a_near, a_far = send(a, Y_NEAR), send(a, Y_FAR)
    near_z = send(far_z, Z_NEAR)
    near_z, q_other = lax.optimization_barrier((near_z, q_other))
    b = jnp.concatenate([near_z, send(near_z, Z_FAR)], axis=0)
    b_near, b_far = send(b, Y_NEAR), send(b, Y_FAR)
    a_last = send(a_near, Y_FAR)

    def block_row(chip_y):
        return jnp.where(diagonal, chip_y % NY, NY - 1 - chip_y % NY)

    own_row = block_row(y)
    other_rows = NY - 1 - own_row + jnp.where(c == 0, 1, 0)
    info = jnp.stack([own_row, other_rows, own_row, jnp.int32(-1), z, diagonal, c, 2 * X, 2 - 2 * X]).astype(jnp.int32)
    near, far, last = block_row(y + sy), block_row(y - sy), block_row(y - 2 * sy)
    rows = jnp.stack([own_row, near, far, own_row, near, last, far, last]).astype(jnp.int32)
    z_a = [z, z + sz, z - sz, z - 2 * sz]
    z_b = [z + 2 * sz, z + 3 * sz, z - 3 * sz, z - 4 * sz]
    zs = jnp.stack([w % NZ for w in z_a * 3 + z_b * 2 + z_a + z_b * 2]).astype(jnp.int32)
    q = jnp.concatenate([q_own, q_other], axis=0)

    early = [a, a_near, a_far]
    state = attend_pieces(info, rows, zs, q, lax.optimization_barrier((early, b))[0], 0)
    b_near, state = lax.optimization_barrier((b_near, state))
    b_last = send(b_near, Y_FAR)
    middle = [b, b_near, a_last, b_far]
    state = attend_pieces(info, rows, zs, q, middle, 3, state)
    pieces = early + middle + [b_last]
    keep, give = attend_last(info, rows, zs, q, state, pieces)
    home = merge(keep, send(give, CORE))
    home, out_weight = lax.optimization_barrier((home, out_weight))
    w_far = load_columns(info, out_weight, 8)
    away = send(home, SWAP_BACK)

    far_give, far_keep = project(info, home, away, w_far)
    far = (far_keep + send(far_give, CORE).astype(jnp.float32)).astype(jnp.bfloat16)
    home, out_weight, far = lax.optimization_barrier((home, out_weight, far))
    far = send(far, XHI)
    near_give, near_keep = project(info, home, away, load_columns(info, out_weight, 7))
    near = near_keep + send(near_give, CORE).astype(jnp.float32)
    return (near + far.astype(jnp.float32)).astype(jnp.bfloat16)


def solution(mesh):
    in_specs = (
        P("seq", "head", None),
        P("seq", "head", None),
        P("seq", "head", None),
        P("head", None),
    )
    out_specs = P("seq", "head")
    return jax.shard_map(
        on_device, mesh=mesh, in_specs=in_specs, out_specs=out_specs, check_vma=False
    )
```

```python
import functools
import math

import jax
import jax.numpy as jnp
from jax import lax
from jax.experimental import pallas as pl
from jax.experimental.pallas import tpu as pltpu
from jax.sharding import PartitionSpec as P

NY, NX, NZ = 4, 2, 8
TOK = 256
HEADS = 8
HD = 128
ROWS = TOK * HEADS
DEEP = HD + 16
SLOTS = NY * NZ
KEYS = SLOTS * TOK
KT = 1024
RC = 512
PER_TILE = KT // TOK
SCALE2 = math.log2(math.e) / math.sqrt(HD)
LOW, HIGH = 1e-20, 1e34
NEG = -1e30
AXES = ("seq", "head")
BOTH = (((1,), (1,)), ((), ()))


def device(X, y, x, z, c):
    return ((y % NY) * 16 + x * 8 + z % NZ) * 4 + X * 2 + c


def perm_of(f):
    return [
        (device(X, y, x, z, c), device(*f(X, y, x, z, c)))
        for y in range(NY)
        for x in range(NX)
        for z in range(NZ)
        for X in range(2)
        for c in range(2)
    ]


def sign_of(pos, c):
    return 1 - 2 * ((pos + c) % 2)


SWAP = perm_of(lambda X, y, x, z, c: (X, y, x, z, c) if c == x else (X, 3 - y, 1 - x, z, 1 - c))
SWAP_BACK = [pair for pair in SWAP if pair[0] != pair[1]]
CORE = perm_of(lambda X, y, x, z, c: (X, y, x, z, 1 - c))
XHI = perm_of(lambda X, y, x, z, c: (1 - X, y, x, z, c))
Z_NEAR = perm_of(lambda X, y, x, z, c: (X, y, x, z + sign_of(z, c), c))
Z_FAR = perm_of(lambda X, y, x, z, c: (X, y, x, z - sign_of(z, c), c))
Z_SKIP = perm_of(lambda X, y, x, z, c: (X, y, x, z + 2 * sign_of(z, c), c))
Y_NEAR = perm_of(lambda X, y, x, z, c: (X, y + sign_of(y, c), x, z, c))
Y_FAR = perm_of(lambda X, y, x, z, c: (X, y - sign_of(y, c), x, z, c))


def send(value, perm):
    return lax.ppermute(value, AXES, perm)


def score(k, q):
    return lax.dot_general(k, q, BOTH, preferred_element_type=jnp.float32) * SCALE2


def mask_tile(s, aheads):
    key = lax.broadcasted_iota(jnp.int32, (TOK, RC), 0)
    tok = lax.broadcasted_iota(jnp.int32, (TOK, RC), 1) % TOK
    parts = []
    for i, ahead in enumerate(aheads):
        parts.append(jnp.where(key <= tok + ahead, s[i * TOK : (i + 1) * TOK, :], NEG))
    return jnp.concatenate(parts, axis=0)


def fast_tile(q_ref, k_ref, v_ref, acc, block, t, aheads):
    k, v = k_ref[t], v_ref[t]
    s = score(k, q_ref[block, :RC, :])
    for r in range(0, ROWS, RC):
        if aheads is not None:
            s = mask_tile(s, aheads)
        p = jnp.exp2(s).astype(jnp.bfloat16)
        if r + RC < ROWS:
            s = score(k, q_ref[block, r + RC : r + 2 * RC, :])
        acc[block, :, r : r + RC] += jnp.dot(v, p, preferred_element_type=jnp.float32)


def slow_tile(q_ref, k_ref, v_ref, acc, top, block, t, aheads):
    def chunk(r, _):
        at = pl.ds(pl.multiple_of(r * RC, RC), RC)
        s = mask_tile(score(k_ref[t], q_ref[block, at, :]), aheads)
        old = top[:1, at]
        new = jnp.maximum(old, jnp.max(s, axis=0, keepdims=True))
        p = jnp.exp2(s - new).astype(jnp.bfloat16)
        sums = jnp.dot(v_ref[t], p, preferred_element_type=jnp.float32)
        acc[block, :, at] = acc[block, :, at] * jnp.exp2(old - new) + sums
        top[:, at] = jnp.broadcast_to(new, (8, RC))
        return 0

    lax.fori_loop(0, ROWS // RC, chunk, 0)


def tiles(run, info, rows, zs, first, n_tiles, base, block, split):
    def step(t, _):
        at = (first + t) * PER_TILE
        row = rows[first + t]
        nearest = zs[at]
        for i in range(1, PER_TILE):
            nearest = jnp.minimum(nearest, zs[at + i])
        whole = row < info[block]
        part = jnp.logical_and(row == info[2 + block], nearest <= info[4])
        aheads = [(info[4] - zs[at + i]) * TOK for i in range(PER_TILE)]
        if split:
            pl.when(whole)(lambda: run(base + t, None))
            pl.when(part)(lambda: run(base + t, aheads))
        else:
            aheads = [jnp.where(whole, TOK, ahead) for ahead in aheads]
            pl.when(jnp.logical_or(whole, part))(lambda: run(base + t, aheads))
        return 0

    lax.fori_loop(0, n_tiles, step, 0)


def place(piece, k_ref, v_ref, t):
    for i in range(PER_TILE):
        src, dst = 2 * i * TOK, i * TOK
        k_ref[t, dst : dst + TOK, :] = piece[src : src + TOK, :]
        for j in range(0, TOK, HD):
            values = piece[src + TOK + j : src + TOK + j + HD, :]
            v_ref[t, :HD, dst + j : dst + j + HD] = values
    v_ref[t, HD:, :] = jnp.ones((DEEP - HD, KT), jnp.bfloat16)


def fast_blocks(info, rows, zs, first, n_tiles, base, q_ref, k_ref, v_ref, acc):
    def block_step(block, _):
        def run(t, aheads):
            fast_tile(q_ref, k_ref, v_ref, acc, block, t, aheads)

        tiles(run, info, rows, zs, first, n_tiles, base, block, True)
        return 0

    lax.fori_loop(0, 2, block_step, 0)


def piece_kernel(first, n_tiles, has_state, info, rows, zs, q_ref, *refs):
    pieces, refs = refs[:n_tiles], refs[n_tiles:]
    acc, k_ref, v_ref = refs[-3:]
    if not has_state:
        acc[...] = jnp.zeros_like(acc)
    for t, piece in enumerate(pieces):
        place(piece, k_ref, v_ref, t)
    fast_blocks(info, rows, zs, first, n_tiles, 0, q_ref, k_ref, v_ref, acc)


def tile_scratch(n):
    return [pltpu.VMEM((n, KT, HD), jnp.bfloat16), pltpu.VMEM((n, DEEP, KT), jnp.bfloat16)]


VMEM = pl.BlockSpec(memory_space=pltpu.VMEM)
SMEM = pl.BlockSpec(memory_space=pltpu.SMEM)
STATE = jax.ShapeDtypeStruct((2, DEEP, ROWS), jnp.float32)
PART = jax.ShapeDtypeStruct((DEEP, ROWS), jnp.float32)


def cost(n_tiles):
    return pl.CostEstimate(
        flops=8 * n_tiles * ROWS * KT * HD,
        bytes_accessed=4 * 2**20,
        transcendentals=n_tiles * ROWS * KT,
    )


def attend_pieces(info, rows, zs, q, pieces, first, state=None):
    n_tiles = len(pieces)
    extra = [] if state is None else [state]
    return pl.pallas_call(
        functools.partial(piece_kernel, first, n_tiles, state is not None),
        out_shape=STATE,
        in_specs=[SMEM, SMEM, SMEM, VMEM] + [VMEM] * (n_tiles + len(extra)),
        out_specs=VMEM,
        scratch_shapes=tile_scratch(n_tiles),
        compiler_params=pltpu.CompilerParams(vmem_limit_bytes=20 * 2**20),
        input_output_aliases={} if state is None else {4 + n_tiles: 0},
        cost_estimate=cost(n_tiles),
        name=f"attend_{first}",
    )(info, rows, zs, q, *pieces, *extra)


def last_kernel(n_pieces, info, rows, zs, q_ref, state, *refs):
    pieces = refs[:n_pieces]
    acc, keep_ref, give_ref, k_ref, v_ref, top = refs[n_pieces:]
    last = n_pieces - 1
    place(pieces[last], k_ref, v_ref, last)
    fast_blocks(info, rows, zs, last, 1, last, q_ref, k_ref, v_ref, acc)
    for block, out_ref in enumerate((keep_ref, give_ref)):
        total = acc[block, HD : HD + 8, :]
        bad = jnp.logical_not(jnp.logical_and(total >= LOW, total <= HIGH))
        n_bad = jnp.sum(jnp.max(bad.astype(jnp.float32), axis=0, keepdims=True))
        some = jnp.logical_or(info[block] > 0, info[2 + block] >= 0)
        out_ref[HD + 8 :, :] = jnp.full((8, ROWS), jnp.where(some, 0.0, NEG), jnp.float32)

        @pl.when(jnp.logical_and(some, n_bad > 0.0))
        def _(block=block, out_ref=out_ref):
            acc[block] = jnp.zeros((DEEP, ROWS), jnp.float32)
            top[...] = jnp.full((8, ROWS), NEG, jnp.float32)
            for t, piece in enumerate(pieces[:last]):
                place(piece, k_ref, v_ref, t)

            def run(t, aheads):
                slow_tile(q_ref, k_ref, v_ref, acc, top, block, t, aheads)

            tiles(run, info, rows, zs, 0, n_pieces, 0, block, False)
            out_ref[HD + 8 :, :] = top[...]

        out_ref[: HD + 8, :] = acc[block, : HD + 8, :]


def attend_last(info, rows, zs, q, state, pieces):
    return pl.pallas_call(
        functools.partial(last_kernel, len(pieces)),
        out_shape=(STATE, PART, PART),
        in_specs=[SMEM, SMEM, SMEM] + [VMEM] * (2 + len(pieces)),
        out_specs=(VMEM, VMEM, VMEM),
        scratch_shapes=tile_scratch(len(pieces)) + [pltpu.VMEM((8, ROWS), jnp.float32)],
        input_output_aliases={4: 0},
        compiler_params=pltpu.CompilerParams(vmem_limit_bytes=20 * 2**20),
        cost_estimate=cost(1),
        name="attend_last",
    )(info, rows, zs, q, state, *pieces)[1:]


def merge_kernel(a_ref, b_ref, out_ref):
    sums, tops = slice(HD, HD + 1), slice(HD + 8, HD + 9)
    top = jnp.maximum(a_ref[tops, :], b_ref[tops, :])
    fa, fb = jnp.exp2(a_ref[tops, :] - top), jnp.exp2(b_ref[tops, :] - top)
    total = a_ref[sums, :] * fa + b_ref[sums, :] * fb
    fa, fb = fa / total, fb / total
    for h in range(HEADS):
        at = slice(h * TOK, (h + 1) * TOK)
        value = a_ref[:HD, at] * fa[:, at] + b_ref[:HD, at] * fb[:, at]
        out_ref[:, h * HD : (h + 1) * HD] = value.T.astype(jnp.bfloat16)


def merge(a, b):
    return pl.pallas_call(
        merge_kernel,
        out_shape=jax.ShapeDtypeStruct((TOK, HEADS * HD), jnp.bfloat16),
        in_specs=[VMEM, VMEM],
        out_specs=VMEM,
        compiler_params=pltpu.CompilerParams(vmem_limit_bytes=8 * 2**20),
        name="merge",
    )(a, b)


def pack_kernel(k_ref, v_ref, out_ref):
    out_ref[:TOK, :] = k_ref[...]
    for j in range(0, TOK, HD):
        out_ref[TOK + j : TOK + j + HD, :] = v_ref[j : j + HD, :].T


def pack(k, v):
    return pl.pallas_call(
        pack_kernel, out_shape=jax.ShapeDtypeStruct((2 * TOK, HD), jnp.bfloat16), name="pack"
    )(k, v)


COLS = 512
SLICE = 1024


def load_kernel(first, info, w_ref, out_ref, sem):
    col = pl.multiple_of(info[first] * SLICE, SLICE)
    copy = pltpu.make_async_copy(w_ref.at[:, pl.ds(col, 2 * SLICE)], out_ref, sem)
    copy.start()
    copy.wait()


def load_columns(info, w, first):
    return pl.pallas_call(
        functools.partial(load_kernel, first),
        out_shape=jax.ShapeDtypeStruct((w.shape[0], 2 * SLICE), w.dtype),
        in_specs=[SMEM, pl.BlockSpec(memory_space=pltpu.HBM)],
        out_specs=VMEM,
        scratch_shapes=[pltpu.SemaphoreType.DMA],
        compiler_params=pltpu.CompilerParams(vmem_limit_bytes=4 * 2**20),
        cost_estimate=pl.CostEstimate(flops=0, bytes_accessed=2**23, transcendentals=0),
        name=f"load_{first}",
    )(info, w)


def project_kernel(info, home_ref, away_ref, w_ref, give_ref, keep_ref, x_ref):
    x_ref[...] = home_ref[...]

    @pl.when(info[5] == 0)
    def _():
        x_ref[...] = away_ref[...]

    for out_ref, side in ((give_ref, 1 - info[6]), (keep_ref, info[6])):
        for j in range(0, SLICE, COLS):
            at = pl.ds(pl.multiple_of(side * SLICE + j, COLS), COLS)
            value = jnp.dot(x_ref[...], w_ref[:, at], preferred_element_type=jnp.float32)
            out_ref[:, j : j + COLS] = value.astype(out_ref.dtype)


def project(info, home, away, w):
    return pl.pallas_call(
        project_kernel,
        out_shape=(
            jax.ShapeDtypeStruct((TOK, SLICE), jnp.bfloat16),
            jax.ShapeDtypeStruct((TOK, SLICE), jnp.float32),
        ),
        in_specs=[SMEM, VMEM, VMEM, VMEM],
        out_specs=(VMEM, VMEM),
        scratch_shapes=[pltpu.VMEM((TOK, SLICE), jnp.bfloat16)],
        compiler_params=pltpu.CompilerParams(vmem_limit_bytes=8 * 2**20),
        name="project",
    )(info, home, away, w)


def on_device(queries, key_states, value_vectors_all, out_weight):
    seq = lax.axis_index("seq")
    head = lax.axis_index("head")
    y, x, z = seq // 16, (seq // 8) % 2, seq % 8
    X, c = head // 2, head % 2
    diagonal = c == x

    k = key_states.reshape(TOK, HD)
    v = value_vectors_all.reshape(TOK, HD)
    kv = send(pack(k, v), SWAP)
    q = queries.transpose(1, 0, 2).reshape(ROWS, HD)

    sz, sy = sign_of(z, c), sign_of(y, c)
    near_z, far_z, skip_z = send(kv, Z_NEAR), send(kv, Z_FAR), send(kv, Z_SKIP)
    near_z, far_z, skip_z, q = lax.optimization_barrier((near_z, far_z, skip_z, q))
    q_own = send(q, SWAP)
    side = jnp.concatenate([far_z, skip_z], axis=0)
    a = jnp.concatenate([kv, near_z, side], axis=0)
    a_near, a_far = send(a, Y_NEAR), send(a, Y_FAR)
    b = jnp.concatenate([send(side, Z_NEAR), send(side, Z_SKIP)], axis=0)
    b_near, b_far = send(b, Y_NEAR), send(b, Y_FAR)
    a_near, b = lax.optimization_barrier((a_near, b))
    a_last = send(a_near, Y_FAR)
    q_own, b = lax.optimization_barrier((q_own, b))
    q_other = send(q_own, CORE)

    def block_row(chip_y):
        return jnp.where(diagonal, chip_y % NY, NY - 1 - chip_y % NY)

    own_row = block_row(y)
    other_rows = NY - 1 - own_row + jnp.where(c == 0, 1, 0)
    info = jnp.stack([own_row, other_rows, own_row, jnp.int32(-1), z, diagonal, c, 2 * X, 2 - 2 * X]).astype(jnp.int32)
    near, far, last = block_row(y + sy), block_row(y - sy), block_row(y - 2 * sy)
    rows = jnp.stack([own_row, near, far, own_row, near, last, far, last]).astype(jnp.int32)
    z_a = [z, z + sz, z - sz, z - 2 * sz]
    z_b = [z + 2 * sz, z + 3 * sz, z - 3 * sz, z - 4 * sz]
    zs = jnp.stack([w % NZ for w in z_a * 3 + z_b * 2 + z_a + z_b * 2]).astype(jnp.int32)
    q = jnp.stack([q_own, q_other])

    early = [a, a_near, a_far]
    state = attend_pieces(info, rows, zs, q, lax.optimization_barrier((early, b))[0], 0)
    b_near, state = lax.optimization_barrier((b_near, state))
    b_last = send(b_near, Y_FAR)
    middle = [b, b_near, a_last, b_far]
    state = attend_pieces(info, rows, zs, q, middle, 3, state)
    pieces = early + middle + [b_last]
    keep, give = attend_last(info, rows, zs, q, state, pieces)
    home = merge(keep, send(give, CORE))
    home, out_weight = lax.optimization_barrier((home, out_weight))
    w_far = load_columns(info, out_weight, 8)
    away = send(home, SWAP_BACK)

    far_give, far_keep = project(info, home, away, w_far)
    far = (far_keep + send(far_give, CORE).astype(jnp.float32)).astype(jnp.bfloat16)
    home, out_weight, far = lax.optimization_barrier((home, out_weight, far))
    far = send(far, XHI)
    near_give, near_keep = project(info, home, away, load_columns(info, out_weight, 7))
    near = near_keep + send(near_give, CORE).astype(jnp.float32)
    return (near + far.astype(jnp.float32)).astype(jnp.bfloat16)


def solution(mesh):
    in_specs = (
        P("seq", "head", None),
        P("seq", "head", None),
        P("seq", "head", None),
        P("head", None),
    )
    out_specs = P("seq", "head")
    return jax.shard_map(
        on_device, mesh=mesh, in_specs=in_specs, out_specs=out_specs, check_vma=False
    )
```

```python
import functools
import math

import jax
import jax.numpy as jnp
from jax import lax
from jax.experimental import pallas as pl
from jax.experimental.pallas import tpu as pltpu
from jax.sharding import PartitionSpec as P

NY, NX, NZ = 4, 2, 8
TOK = 256
HEADS = 8
HD = 128
ROWS = TOK * HEADS
DEEP = HD + 16
SLOTS = NY * NZ
KEYS = SLOTS * TOK
KT = 1024
RC = 512
PER_TILE = KT // TOK
SCALE2 = math.log2(math.e) / math.sqrt(HD)
LOW, HIGH = 1e-20, 1e34
NEG = -1e30
AXES = ("seq", "head")
BOTH = (((1,), (1,)), ((), ()))


def device(X, y, x, z, c):
    return ((y % NY) * 16 + x * 8 + z % NZ) * 4 + X * 2 + c


def perm_of(f):
    return [
        (device(X, y, x, z, c), device(*f(X, y, x, z, c)))
        for y in range(NY)
        for x in range(NX)
        for z in range(NZ)
        for X in range(2)
        for c in range(2)
    ]


def sign_of(pos, c):
    return 1 - 2 * ((pos + c) % 2)


SWAP = perm_of(lambda X, y, x, z, c: (X, y, x, z, c) if c == x else (X, 3 - y, 1 - x, z, 1 - c))
KV_SWAP = perm_of(lambda X, y, x, z, c: (X, y, x, z, c) if c == x else (X, y, 1 - x, z, 1 - c))
SWAP_BACK = [pair for pair in SWAP if pair[0] != pair[1]]
CORE = perm_of(lambda X, y, x, z, c: (X, y, x, z, 1 - c))
XHI = perm_of(lambda X, y, x, z, c: (1 - X, y, x, z, c))
Z_NEAR = perm_of(lambda X, y, x, z, c: (X, y, x, z + sign_of(z, c), c))
Z_FAR = perm_of(lambda X, y, x, z, c: (X, y, x, z - sign_of(z, c), c))
Z_SKIP = perm_of(lambda X, y, x, z, c: (X, y, x, z + 2 * sign_of(z, c), c))
Y_NEAR = perm_of(lambda X, y, x, z, c: (X, y + sign_of(y, c), x, z, c))
Y_FAR = perm_of(lambda X, y, x, z, c: (X, y - sign_of(y, c), x, z, c))


def send(value, perm):
    return lax.ppermute(value, AXES, perm)


def score(k, q):
    return lax.dot_general(k, q, BOTH, preferred_element_type=jnp.float32) * SCALE2


def mask_tile(s, aheads):
    key = lax.broadcasted_iota(jnp.int32, (TOK, RC), 0)
    tok = lax.broadcasted_iota(jnp.int32, (TOK, RC), 1) % TOK
    parts = []
    for i, ahead in enumerate(aheads):
        parts.append(jnp.where(key <= tok + ahead, s[i * TOK : (i + 1) * TOK, :], NEG))
    return jnp.concatenate(parts, axis=0)


def fast_tile(q_ref, k_ref, v_ref, acc, block, t, aheads):
    k, v = k_ref[t], v_ref[t]
    s = score(k, q_ref[block, :RC, :])
    for r in range(0, ROWS, RC):
        if aheads is not None:
            s = mask_tile(s, aheads)
        p = jnp.exp2(s).astype(jnp.bfloat16)
        if r + RC < ROWS:
            s = score(k, q_ref[block, r + RC : r + 2 * RC, :])
        acc[block, :, r : r + RC] += jnp.dot(v, p, preferred_element_type=jnp.float32)


def slow_tile(q_ref, k_ref, v_ref, acc, top, block, t, aheads):
    def chunk(r, _):
        at = pl.ds(pl.multiple_of(r * RC, RC), RC)
        s = mask_tile(score(k_ref[t], q_ref[block, at, :]), aheads)
        old = top[:1, at]
        new = jnp.maximum(old, jnp.max(s, axis=0, keepdims=True))
        p = jnp.exp2(s - new).astype(jnp.bfloat16)
        sums = jnp.dot(v_ref[t], p, preferred_element_type=jnp.float32)
        acc[block, :, at] = acc[block, :, at] * jnp.exp2(old - new) + sums
        top[:, at] = jnp.broadcast_to(new, (8, RC))
        return 0

    lax.fori_loop(0, ROWS // RC, chunk, 0)


def tiles(run, info, rows, zs, first, n_tiles, base, block, split):
    def step(t, _):
        at = (first + t) * PER_TILE
        row = rows[first + t]
        nearest = zs[at]
        for i in range(1, PER_TILE):
            nearest = jnp.minimum(nearest, zs[at + i])
        whole = row < info[block]
        part = jnp.logical_and(row == info[2 + block], nearest <= info[4])
        aheads = [(info[4] - zs[at + i]) * TOK for i in range(PER_TILE)]
        if split:
            pl.when(whole)(lambda: run(base + t, None))
            pl.when(part)(lambda: run(base + t, aheads))
        else:
            aheads = [jnp.where(whole, TOK, ahead) for ahead in aheads]
            pl.when(jnp.logical_or(whole, part))(lambda: run(base + t, aheads))
        return 0

    lax.fori_loop(0, n_tiles, step, 0)


def place(piece, k_ref, v_ref, t):
    for i in range(PER_TILE):
        src, dst = 2 * i * TOK, i * TOK
        k_ref[t, dst : dst + TOK, :] = piece[src : src + TOK, :]
        for j in range(0, TOK, HD):
            values = piece[src + TOK + j : src + TOK + j + HD, :]
            v_ref[t, :HD, dst + j : dst + j + HD] = values
    v_ref[t, HD:, :] = jnp.ones((DEEP - HD, KT), jnp.bfloat16)


def fast_blocks(info, rows, zs, first, n_tiles, base, q_ref, k_ref, v_ref, acc):
    def block_step(block, _):
        def run(t, aheads):
            fast_tile(q_ref, k_ref, v_ref, acc, block, t, aheads)

        tiles(run, info, rows, zs, first, n_tiles, base, block, True)
        return 0

    lax.fori_loop(0, 2, block_step, 0)


def piece_kernel(first, n_tiles, has_state, info, rows, zs, q_ref, *refs):
    pieces, refs = refs[:n_tiles], refs[n_tiles:]
    acc, k_ref, v_ref = refs[-3:]
    if not has_state:
        acc[...] = jnp.zeros_like(acc)
    for t, piece in enumerate(pieces):
        place(piece, k_ref, v_ref, t)
    fast_blocks(info, rows, zs, first, n_tiles, 0, q_ref, k_ref, v_ref, acc)


def tile_scratch(n):
    return [pltpu.VMEM((n, KT, HD), jnp.bfloat16), pltpu.VMEM((n, DEEP, KT), jnp.bfloat16)]


VMEM = pl.BlockSpec(memory_space=pltpu.VMEM)
SMEM = pl.BlockSpec(memory_space=pltpu.SMEM)
STATE = jax.ShapeDtypeStruct((2, DEEP, ROWS), jnp.float32)
PART = jax.ShapeDtypeStruct((DEEP, ROWS), jnp.float32)
GIVEN = jax.ShapeDtypeStruct((DEEP, ROWS), jnp.bfloat16)


def cost(n_tiles):
    return pl.CostEstimate(
        flops=8 * n_tiles * ROWS * KT * HD,
        bytes_accessed=4 * 2**20,
        transcendentals=n_tiles * ROWS * KT,
    )


def attend_pieces(info, rows, zs, q, pieces, first, state=None):
    n_tiles = len(pieces)
    extra = [] if state is None else [state]
    return pl.pallas_call(
        functools.partial(piece_kernel, first, n_tiles, state is not None),
        out_shape=STATE,
        in_specs=[SMEM, SMEM, SMEM, VMEM] + [VMEM] * (n_tiles + len(extra)),
        out_specs=VMEM,
        scratch_shapes=tile_scratch(n_tiles),
        compiler_params=pltpu.CompilerParams(vmem_limit_bytes=20 * 2**20),
        input_output_aliases={} if state is None else {4 + n_tiles: 0},
        cost_estimate=cost(n_tiles),
        name=f"attend_{first}",
    )(info, rows, zs, q, *pieces, *extra)


def in_parts(row, n):
    parts = []
    for _ in range(n):
        parts.append(row.astype(jnp.bfloat16).astype(jnp.float32))
        row = row - parts[-1]
    return parts


def last_kernel(n_pieces, info, rows, zs, q_ref, state, *refs):
    pieces = refs[:n_pieces]
    acc, keep_ref, give_ref, k_ref, v_ref, top = refs[n_pieces:]
    last = n_pieces - 1
    place(pieces[last], k_ref, v_ref, last)
    fast_blocks(info, rows, zs, last, 1, last, q_ref, k_ref, v_ref, acc)
    for block in range(2):
        total = acc[block, HD : HD + 8, :]
        bad = jnp.logical_not(jnp.logical_and(total >= LOW, total <= HIGH))
        n_bad = jnp.sum(jnp.max(bad.astype(jnp.float32), axis=0, keepdims=True))
        some = jnp.logical_or(info[block] > 0, info[2 + block] >= 0)
        top[...] = jnp.full((8, ROWS), jnp.where(some, 0.0, NEG), jnp.float32)

        @pl.when(jnp.logical_and(some, n_bad > 0.0))
        def _(block=block):
            acc[block] = jnp.zeros((DEEP, ROWS), jnp.float32)
            top[...] = jnp.full((8, ROWS), NEG, jnp.float32)
            for t, piece in enumerate(pieces[:last]):
                place(piece, k_ref, v_ref, t)

            def run(t, aheads):
                slow_tile(q_ref, k_ref, v_ref, acc, top, block, t, aheads)

            tiles(run, info, rows, zs, 0, n_pieces, 0, block, False)

        if block == 0:
            keep_ref[: HD + 8, :] = acc[block, : HD + 8, :]
            keep_ref[HD + 8 :, :] = top[...]
        else:
            give_ref[:HD, :] = acc[block, :HD, :].astype(jnp.bfloat16)
            parts = in_parts(acc[block, HD : HD + 1, :], 2) + in_parts(top[:1, :], 3)
            row = lax.broadcasted_iota(jnp.int32, (DEEP - HD, ROWS), 0)
            ends = jnp.zeros((DEEP - HD, ROWS), jnp.float32)
            for i, part in enumerate(parts):
                ends = jnp.where(row == i, part, ends)
            give_ref[HD:, :] = ends.astype(jnp.bfloat16)


def attend_last(info, rows, zs, q, state, pieces):
    return pl.pallas_call(
        functools.partial(last_kernel, len(pieces)),
        out_shape=(STATE, PART, GIVEN),
        in_specs=[SMEM, SMEM, SMEM] + [VMEM] * (2 + len(pieces)),
        out_specs=(VMEM, VMEM, VMEM),
        scratch_shapes=tile_scratch(len(pieces)) + [pltpu.VMEM((8, ROWS), jnp.float32)],
        input_output_aliases={4: 0},
        compiler_params=pltpu.CompilerParams(vmem_limit_bytes=20 * 2**20),
        cost_estimate=cost(1),
        name="attend_last",
    )(info, rows, zs, q, state, *pieces)[1:]


def merge_kernel(a_ref, b_ref, out_ref):
    a_sum, a_top = a_ref[HD : HD + 1, :], a_ref[HD + 8 : HD + 9, :]
    ends = b_ref[HD:, :].astype(jnp.float32)
    b_sum = ends[0:1] + ends[1:2]
    b_top = ends[2:3] + ends[3:4] + ends[4:5]
    top = jnp.maximum(a_top, b_top)
    fa, fb = jnp.exp2(a_top - top), jnp.exp2(b_top - top)
    total = a_sum * fa + b_sum * fb
    fa, fb = fa / total, fb / total
    for h in range(HEADS):
        at = slice(h * TOK, (h + 1) * TOK)
        value = a_ref[:HD, at] * fa[:, at] + b_ref[:HD, at].astype(jnp.float32) * fb[:, at]
        out_ref[:, h * HD : (h + 1) * HD] = value.T.astype(jnp.bfloat16)


def merge(a, b):
    return pl.pallas_call(
        merge_kernel,
        out_shape=jax.ShapeDtypeStruct((TOK, HEADS * HD), jnp.bfloat16),
        in_specs=[VMEM, VMEM],
        out_specs=VMEM,
        compiler_params=pltpu.CompilerParams(vmem_limit_bytes=8 * 2**20),
        name="merge",
    )(a, b)


def pack_kernel(k_ref, v_ref, out_ref):
    out_ref[:TOK, :] = k_ref[...]
    for j in range(0, TOK, HD):
        out_ref[TOK + j : TOK + j + HD, :] = v_ref[j : j + HD, :].T


def pack(k, v):
    return pl.pallas_call(
        pack_kernel, out_shape=jax.ShapeDtypeStruct((2 * TOK, HD), jnp.bfloat16), name="pack"
    )(k, v)


COLS = 512
SLICE = 1024


def load_kernel(first, info, w_ref, out_ref, sem):
    col = pl.multiple_of(info[first] * SLICE, SLICE)
    copy = pltpu.make_async_copy(w_ref.at[:, pl.ds(col, 2 * SLICE)], out_ref, sem)
    copy.start()
    copy.wait()


def load_columns(info, w, first):
    return pl.pallas_call(
        functools.partial(load_kernel, first),
        out_shape=jax.ShapeDtypeStruct((w.shape[0], 2 * SLICE), w.dtype),
        in_specs=[SMEM, pl.BlockSpec(memory_space=pltpu.HBM)],
        out_specs=VMEM,
        scratch_shapes=[pltpu.SemaphoreType.DMA],
        compiler_params=pltpu.CompilerParams(vmem_limit_bytes=4 * 2**20),
        cost_estimate=pl.CostEstimate(flops=0, bytes_accessed=2**23, transcendentals=0),
        name=f"load_{first}",
    )(info, w)


def project_kernel(info, home_ref, away_ref, w_ref, give_ref, keep_ref, x_ref):
    x_ref[...] = home_ref[...]

    @pl.when(info[5] == 0)
    def _():
        x_ref[...] = away_ref[...]

    for out_ref, side in ((give_ref, 1 - info[6]), (keep_ref, info[6])):
        for j in range(0, SLICE, COLS):
            at = pl.ds(pl.multiple_of(side * SLICE + j, COLS), COLS)
            value = jnp.dot(x_ref[...], w_ref[:, at], preferred_element_type=jnp.float32)
            out_ref[:, j : j + COLS] = value.astype(out_ref.dtype)


def project(info, home, away, w):
    return pl.pallas_call(
        project_kernel,
        out_shape=(
            jax.ShapeDtypeStruct((TOK, SLICE), jnp.bfloat16),
            jax.ShapeDtypeStruct((TOK, SLICE), jnp.float32),
        ),
        in_specs=[SMEM, VMEM, VMEM, VMEM],
        out_specs=(VMEM, VMEM),
        scratch_shapes=[pltpu.VMEM((TOK, SLICE), jnp.bfloat16)],
        compiler_params=pltpu.CompilerParams(vmem_limit_bytes=8 * 2**20),
        name="project",
    )(info, home, away, w)


def on_device(queries, key_states, value_vectors_all, out_weight):
    seq = lax.axis_index("seq")
    head = lax.axis_index("head")
    y, x, z = seq // 16, (seq // 8) % 2, seq % 8
    X, c = head // 2, head % 2
    diagonal = c == x

    k = key_states.reshape(TOK, HD)
    v = value_vectors_all.reshape(TOK, HD)
    kv = send(pack(k, v), KV_SWAP)
    q = queries.transpose(1, 0, 2).reshape(ROWS, HD)

    sz, sy = sign_of(z, c), sign_of(y, c)
    near_z, far_z, skip_z = send(kv, Z_NEAR), send(kv, Z_FAR), send(kv, Z_SKIP)
    near_z, far_z, skip_z, q = lax.optimization_barrier((near_z, far_z, skip_z, q))
    q_own = send(q, SWAP)
    side = jnp.concatenate([far_z, skip_z], axis=0)
    a = jnp.concatenate([kv, near_z, side], axis=0)
    a_near, a_far = send(a, Y_NEAR), send(a, Y_FAR)
    b = jnp.concatenate([send(side, Z_NEAR), send(side, Z_SKIP)], axis=0)
    b_near, b_far = send(b, Y_NEAR), send(b, Y_FAR)
    a_near, a_far, b = lax.optimization_barrier((a_near, a_far, b))
    a_last = send(a_near, Y_FAR)
    q_own, b = lax.optimization_barrier((q_own, b))
    q_other = send(q_own, CORE)

    own_row = jnp.where(diagonal, y, NY - 1 - y)
    other_rows = NY - 1 - own_row + jnp.where(c == 0, 1, 0)
    info = jnp.stack([own_row, other_rows, own_row, jnp.int32(-1), z, diagonal, c, 2 * X, 2 - 2 * X]).astype(jnp.int32)
    near, far, last = y + sy, y - sy, y - 2 * sy
    rows = jnp.stack([w % NY for w in (y, near, far, y, last, near, far, last)]).astype(jnp.int32)
    z_a = [z, z + sz, z - sz, z - 2 * sz]
    z_b = [z + 2 * sz, z + 3 * sz, z - 3 * sz, z - 4 * sz]
    zs = jnp.stack([w % NZ for w in z_a * 3 + z_b + z_a + z_b * 3]).astype(jnp.int32)
    q = jnp.stack([q_own, q_other])

    early = [a, a_near, a_far, b]
    state = attend_pieces(info, rows, zs, q, early, 0)
    b_near, state = lax.optimization_barrier((b_near, state))
    b_last = send(b_near, Y_FAR)
    middle = [a_last, b_near, b_far]
    state = attend_pieces(info, rows, zs, q, middle, 4, state)
    pieces = early + middle + [b_last]
    keep, give = attend_last(info, rows, zs, q, state, pieces)
    home = merge(keep, send(give, CORE))
    home, out_weight = lax.optimization_barrier((home, out_weight))
    w_far = load_columns(info, out_weight, 8)
    away = send(home, SWAP_BACK)

    far_give, far_keep = project(info, home, away, w_far)
    far = (far_keep + send(far_give, CORE).astype(jnp.float32)).astype(jnp.bfloat16)
    home, out_weight, far = lax.optimization_barrier((home, out_weight, far))
    far = send(far, XHI)
    near_give, near_keep = project(info, home, away, load_columns(info, out_weight, 7))
    near = near_keep + send(near_give, CORE).astype(jnp.float32)
    return (near + far.astype(jnp.float32)).astype(jnp.bfloat16)


def solution(mesh):
    in_specs = (
        P("seq", "head", None),
        P("seq", "head", None),
        P("seq", "head", None),
        P("head", None),
    )
    out_specs = P("seq", "head")
    return jax.shard_map(
        on_device, mesh=mesh, in_specs=in_specs, out_specs=out_specs, check_vma=False
    )
```

```python
import functools
import math

import jax
import jax.numpy as jnp
from jax import lax
from jax.experimental import pallas as pl
from jax.experimental.pallas import tpu as pltpu
from jax.sharding import PartitionSpec as P

NY, NX, NZ = 4, 2, 8
TOK = 256
HEADS = 8
HD = 128
ROWS = TOK * HEADS
DEEP = HD + 16
SLOTS = NY * NZ
KEYS = SLOTS * TOK
KT = 1024
RC = 512
PER_TILE = KT // TOK
SCALE2 = math.log2(math.e) / math.sqrt(HD)
LOW, HIGH = 1e-20, 1e34
NEG = -1e30
AXES = ("seq", "head")
BOTH = (((1,), (1,)), ((), ()))


def device(X, y, x, z, c):
    return ((y % NY) * 16 + x * 8 + z % NZ) * 4 + X * 2 + c


def perm_of(f):
    return [
        (device(X, y, x, z, c), device(*f(X, y, x, z, c)))
        for y in range(NY)
        for x in range(NX)
        for z in range(NZ)
        for X in range(2)
        for c in range(2)
    ]


def sign_of(pos, c):
    return 1 - 2 * ((pos + c) % 2)


SWAP = perm_of(lambda X, y, x, z, c: (X, y, x, z, c) if c == x else (X, 3 - y, 1 - x, z, 1 - c))
KV_SWAP = perm_of(lambda X, y, x, z, c: (X, y, x, z, c) if c == x else (X, y, 1 - x, z, 1 - c))
SWAP_BACK = [pair for pair in SWAP if pair[0] != pair[1]]
CORE = perm_of(lambda X, y, x, z, c: (X, y, x, z, 1 - c))
XHI = perm_of(lambda X, y, x, z, c: (1 - X, y, x, z, c))
Z_NEAR = perm_of(lambda X, y, x, z, c: (X, y, x, z + sign_of(z, c), c))
Z_FAR = perm_of(lambda X, y, x, z, c: (X, y, x, z - sign_of(z, c), c))
Z_SKIP = perm_of(lambda X, y, x, z, c: (X, y, x, z + 2 * sign_of(z, c), c))
Y_NEAR = perm_of(lambda X, y, x, z, c: (X, y + sign_of(y, c), x, z, c))
Y_FAR = perm_of(lambda X, y, x, z, c: (X, y - sign_of(y, c), x, z, c))


def send(value, perm):
    return lax.ppermute(value, AXES, perm)


def score(k, q):
    return lax.dot_general(k, q, BOTH, preferred_element_type=jnp.float32) * SCALE2


def mask_tile(s, aheads):
    key = lax.broadcasted_iota(jnp.int32, (TOK, RC), 0)
    tok = lax.broadcasted_iota(jnp.int32, (TOK, RC), 1) % TOK
    parts = []
    for i, ahead in enumerate(aheads):
        parts.append(jnp.where(key <= tok + ahead, s[i * TOK : (i + 1) * TOK, :], NEG))
    return jnp.concatenate(parts, axis=0)


def fast_tile(q_ref, k_ref, v_ref, acc, block, t, aheads):
    k, v = k_ref[t], v_ref[t]
    s = score(k, q_ref[block, :RC, :])
    for r in range(0, ROWS, RC):
        if aheads is not None:
            s = mask_tile(s, aheads)
        p = jnp.exp2(s).astype(jnp.bfloat16)
        if r + RC < ROWS:
            s = score(k, q_ref[block, r + RC : r + 2 * RC, :])
        acc[block, :, r : r + RC] += jnp.dot(v, p, preferred_element_type=jnp.float32)


def slow_tile(q_ref, k_ref, v_ref, acc, top, block, t, aheads):
    def chunk(r, _):
        at = pl.ds(pl.multiple_of(r * RC, RC), RC)
        s = mask_tile(score(k_ref[t], q_ref[block, at, :]), aheads)
        old = top[:1, at]
        new = jnp.maximum(old, jnp.max(s, axis=0, keepdims=True))
        p = jnp.exp2(s - new).astype(jnp.bfloat16)
        sums = jnp.dot(v_ref[t], p, preferred_element_type=jnp.float32)
        acc[block, :, at] = acc[block, :, at] * jnp.exp2(old - new) + sums
        top[:, at] = jnp.broadcast_to(new, (8, RC))
        return 0

    lax.fori_loop(0, ROWS // RC, chunk, 0)


def tiles(run, info, rows, zs, first, n_tiles, base, block, split, skip=0):
    def step(t, _):
        at = (first + t) * PER_TILE
        row = rows[first + t]
        nearest = zs[at]
        for i in range(1, PER_TILE):
            nearest = jnp.minimum(nearest, zs[at + i])
        whole = row < info[block]
        part = jnp.logical_and(row == info[2 + block], nearest <= info[4])
        aheads = [(info[4] - zs[at + i]) * TOK for i in range(PER_TILE)]
        if split:
            pl.when(whole)(lambda: run(base + t, None))
            pl.when(part)(lambda: run(base + t, aheads))
        else:
            aheads = [jnp.where(whole, TOK, ahead) for ahead in aheads]
            pl.when(jnp.logical_or(whole, part))(lambda: run(base + t, aheads))
        return 0

    lax.fori_loop(skip, n_tiles, step, 0)


def place(piece, k_ref, v_ref, t):
    for i in range(PER_TILE):
        src, dst = 2 * i * TOK, i * TOK
        k_ref[t, dst : dst + TOK, :] = piece[src : src + TOK, :]
        for j in range(0, TOK, HD):
            values = piece[src + TOK + j : src + TOK + j + HD, :]
            v_ref[t, :HD, dst + j : dst + j + HD] = values
    v_ref[t, HD:, :] = jnp.ones((DEEP - HD, KT), jnp.bfloat16)


def fast_blocks(info, rows, zs, first, n_tiles, base, q_ref, k_ref, v_ref, acc, skip_own=0):
    def block_step(block, _):
        def run(t, aheads):
            fast_tile(q_ref, k_ref, v_ref, acc, block, t, aheads)

        skip = jnp.where(block == 0, skip_own, 0)
        tiles(run, info, rows, zs, first, n_tiles, base, block, True, skip)
        return 0

    lax.fori_loop(0, q_ref.shape[0], block_step, 0)


def piece_kernel(first, n_tiles, has_state, skip_own, info, rows, zs, q_ref, *refs):
    pieces, refs = refs[:n_tiles], refs[n_tiles:]
    acc, k_ref, v_ref = refs[-3:]
    if not has_state:
        acc[...] = jnp.zeros_like(acc)
    for t, piece in enumerate(pieces):
        place(piece, k_ref, v_ref, t)
    fast_blocks(info, rows, zs, first, n_tiles, 0, q_ref, k_ref, v_ref, acc, skip_own)


def tile_scratch(n):
    return [pltpu.VMEM((n, KT, HD), jnp.bfloat16), pltpu.VMEM((n, DEEP, KT), jnp.bfloat16)]


VMEM = pl.BlockSpec(memory_space=pltpu.VMEM)
SMEM = pl.BlockSpec(memory_space=pltpu.SMEM)
STATE = jax.ShapeDtypeStruct((2, DEEP, ROWS), jnp.float32)
PART = jax.ShapeDtypeStruct((DEEP, ROWS), jnp.float32)
GIVEN = jax.ShapeDtypeStruct((DEEP, ROWS), jnp.bfloat16)


def cost(n_tiles):
    return pl.CostEstimate(
        flops=8 * n_tiles * ROWS * KT * HD,
        bytes_accessed=4 * 2**20,
        transcendentals=n_tiles * ROWS * KT,
    )


def attend_pieces(info, rows, zs, q, pieces, first, state=None, skip_own=0):
    n_tiles = len(pieces)
    extra = [] if state is None else [state]
    return pl.pallas_call(
        functools.partial(piece_kernel, first, n_tiles, state is not None, skip_own),
        out_shape=STATE,
        in_specs=[SMEM, SMEM, SMEM, VMEM] + [VMEM] * (n_tiles + len(extra)),
        out_specs=VMEM,
        scratch_shapes=tile_scratch(n_tiles),
        compiler_params=pltpu.CompilerParams(vmem_limit_bytes=20 * 2**20),
        input_output_aliases={} if state is None else {4 + n_tiles: 0},
        cost_estimate=cost(n_tiles),
        name=f"attend_{first}_{n_tiles}",
    )(info, rows, zs, q, *pieces, *extra)


def in_parts(row, n):
    parts = []
    for _ in range(n):
        parts.append(row.astype(jnp.bfloat16).astype(jnp.float32))
        row = row - parts[-1]
    return parts


def last_kernel(n_pieces, n_last, info, rows, zs, q_ref, state, *refs):
    pieces = refs[:n_pieces]
    acc, keep_ref, give_ref, k_ref, v_ref, top = refs[n_pieces:]
    done = n_pieces - n_last
    for t in range(done, n_pieces):
        place(pieces[t], k_ref, v_ref, t)
    fast_blocks(info, rows, zs, done, n_last, done, q_ref, k_ref, v_ref, acc)
    for block in range(2):
        total = acc[block, HD : HD + 8, :]
        bad = jnp.logical_not(jnp.logical_and(total >= LOW, total <= HIGH))
        n_bad = jnp.sum(jnp.max(bad.astype(jnp.float32), axis=0, keepdims=True))
        some = jnp.logical_or(info[block] > 0, info[2 + block] >= 0)
        top[...] = jnp.full((8, ROWS), jnp.where(some, 0.0, NEG), jnp.float32)

        @pl.when(jnp.logical_and(some, n_bad > 0.0))
        def _(block=block):
            acc[block] = jnp.zeros((DEEP, ROWS), jnp.float32)
            top[...] = jnp.full((8, ROWS), NEG, jnp.float32)
            for t, piece in enumerate(pieces[:done]):
                place(piece, k_ref, v_ref, t)

            def run(t, aheads):
                slow_tile(q_ref, k_ref, v_ref, acc, top, block, t, aheads)

            tiles(run, info, rows, zs, 0, n_pieces, 0, block, False)

        if block == 0:
            keep_ref[: HD + 8, :] = acc[block, : HD + 8, :]
            keep_ref[HD + 8 :, :] = top[...]
        else:
            give_ref[:HD, :] = acc[block, :HD, :].astype(jnp.bfloat16)
            parts = in_parts(acc[block, HD : HD + 1, :], 2) + in_parts(top[:1, :], 3)
            row = lax.broadcasted_iota(jnp.int32, (DEEP - HD, ROWS), 0)
            ends = jnp.zeros((DEEP - HD, ROWS), jnp.float32)
            for i, part in enumerate(parts):
                ends = jnp.where(row == i, part, ends)
            give_ref[HD:, :] = ends.astype(jnp.bfloat16)


def attend_last(info, rows, zs, q, state, pieces, n_last):
    return pl.pallas_call(
        functools.partial(last_kernel, len(pieces), n_last),
        out_shape=(STATE, PART, GIVEN),
        in_specs=[SMEM, SMEM, SMEM] + [VMEM] * (2 + len(pieces)),
        out_specs=(VMEM, VMEM, VMEM),
        scratch_shapes=tile_scratch(len(pieces)) + [pltpu.VMEM((8, ROWS), jnp.float32)],
        input_output_aliases={4: 0},
        compiler_params=pltpu.CompilerParams(vmem_limit_bytes=20 * 2**20),
        cost_estimate=cost(n_last),
        name="attend_last",
    )(info, rows, zs, q, state, *pieces)[1:]


def merge_kernel(a_ref, b_ref, out_ref):
    a_sum, a_top = a_ref[HD : HD + 1, :], a_ref[HD + 8 : HD + 9, :]
    ends = b_ref[HD:, :].astype(jnp.float32)
    b_sum = ends[0:1] + ends[1:2]
    b_top = ends[2:3] + ends[3:4] + ends[4:5]
    top = jnp.maximum(a_top, b_top)
    fa, fb = jnp.exp2(a_top - top), jnp.exp2(b_top - top)
    total = a_sum * fa + b_sum * fb
    fa, fb = fa / total, fb / total
    for h in range(HEADS):
        at = slice(h * TOK, (h + 1) * TOK)
        value = a_ref[:HD, at] * fa[:, at] + b_ref[:HD, at].astype(jnp.float32) * fb[:, at]
        out_ref[:, h * HD : (h + 1) * HD] = value.T.astype(jnp.bfloat16)


def merge(a, b):
    return pl.pallas_call(
        merge_kernel,
        out_shape=jax.ShapeDtypeStruct((TOK, HEADS * HD), jnp.bfloat16),
        in_specs=[VMEM, VMEM],
        out_specs=VMEM,
        compiler_params=pltpu.CompilerParams(vmem_limit_bytes=8 * 2**20),
        name="merge",
    )(a, b)


def pack_kernel(k_ref, v_ref, out_ref):
    out_ref[:TOK, :] = k_ref[...]
    for j in range(0, TOK, HD):
        out_ref[TOK + j : TOK + j + HD, :] = v_ref[j : j + HD, :].T


def pack(k, v):
    return pl.pallas_call(
        pack_kernel, out_shape=jax.ShapeDtypeStruct((2 * TOK, HD), jnp.bfloat16), name="pack"
    )(k, v)


COLS = 512
SLICE = 1024


def load_kernel(first, info, w_ref, out_ref, sem):
    col = pl.multiple_of(info[first] * SLICE, SLICE)
    copy = pltpu.make_async_copy(w_ref.at[:, pl.ds(col, 2 * SLICE)], out_ref, sem)
    copy.start()
    copy.wait()


def load_columns(info, w, first):
    return pl.pallas_call(
        functools.partial(load_kernel, first),
        out_shape=jax.ShapeDtypeStruct((w.shape[0], 2 * SLICE), w.dtype),
        in_specs=[SMEM, pl.BlockSpec(memory_space=pltpu.HBM)],
        out_specs=VMEM,
        scratch_shapes=[pltpu.SemaphoreType.DMA],
        compiler_params=pltpu.CompilerParams(vmem_limit_bytes=4 * 2**20),
        cost_estimate=pl.CostEstimate(flops=0, bytes_accessed=2**23, transcendentals=0),
        name=f"load_{first}",
    )(info, w)


def project_kernel(info, home_ref, away_ref, w_ref, give_ref, keep_ref, x_ref):
    x_ref[...] = home_ref[...]

    @pl.when(info[5] == 0)
    def _():
        x_ref[...] = away_ref[...]

    for out_ref, side in ((give_ref, 1 - info[6]), (keep_ref, info[6])):
        for j in range(0, SLICE, COLS):
            at = pl.ds(pl.multiple_of(side * SLICE + j, COLS), COLS)
            value = jnp.dot(x_ref[...], w_ref[:, at], preferred_element_type=jnp.float32)
            out_ref[:, j : j + COLS] = value.astype(out_ref.dtype)


def project(info, home, away, w):
    return pl.pallas_call(
        project_kernel,
        out_shape=(
            jax.ShapeDtypeStruct((TOK, SLICE), jnp.bfloat16),
            jax.ShapeDtypeStruct((TOK, SLICE), jnp.float32),
        ),
        in_specs=[SMEM, VMEM, VMEM, VMEM],
        out_specs=(VMEM, VMEM),
        scratch_shapes=[pltpu.VMEM((TOK, SLICE), jnp.bfloat16)],
        compiler_params=pltpu.CompilerParams(vmem_limit_bytes=8 * 2**20),
        name="project",
    )(info, home, away, w)


def on_device(queries, key_states, value_vectors_all, out_weight):
    seq = lax.axis_index("seq")
    head = lax.axis_index("head")
    y, x, z = seq // 16, (seq // 8) % 2, seq % 8
    X, c = head // 2, head % 2
    diagonal = c == x

    k = key_states.reshape(TOK, HD)
    v = value_vectors_all.reshape(TOK, HD)
    kv = send(pack(k, v), KV_SWAP)
    q = queries.transpose(1, 0, 2).reshape(ROWS, HD)
    kv, q = lax.optimization_barrier((kv, q))

    sz, sy = sign_of(z, c), sign_of(y, c)
    near_z, far_z, skip_z = send(kv, Z_NEAR), send(kv, Z_FAR), send(kv, Z_SKIP)
    q_own = send(q, SWAP)
    near_z, far_z, skip_z, q_own = lax.optimization_barrier((near_z, far_z, skip_z, q_own))
    side = jnp.concatenate([far_z, skip_z], axis=0)
    a = jnp.concatenate([kv, near_z, side], axis=0)
    a_near, a_far = send(a, Y_NEAR), send(a, Y_FAR)
    own_row = jnp.where(diagonal, y, NY - 1 - y)
    other_rows = NY - 1 - own_row + jnp.where(c == 0, 1, 0)
    info = jnp.stack([own_row, other_rows, own_row, jnp.int32(-1), z, diagonal, c, 2 * X, 2 - 2 * X]).astype(jnp.int32)
    near, far, last = y + sy, y - sy, y - 2 * sy
    rows = jnp.stack([w % NY for w in (y, near, far, y, last, near, far, last)]).astype(jnp.int32)
    z_a = [z, z + sz, z - sz, z - 2 * sz]
    z_b = [z + 2 * sz, z + 3 * sz, z - 3 * sz, z - 4 * sz]
    zs = jnp.stack([w % NZ for w in z_a * 3 + z_b + z_a + z_b * 3]).astype(jnp.int32)
    state = attend_pieces(info, rows, zs, q_own[None], [a], 0)
    b_1, b_2 = send(side, Z_NEAR), send(side, Z_SKIP)
    b_1, b_2, state = lax.optimization_barrier((b_1, b_2, state))
    b = jnp.concatenate([b_1, b_2], axis=0)
    b_near, b_far = send(b, Y_NEAR), send(b, Y_FAR)
    a_near, a_far, b = lax.optimization_barrier((a_near, a_far, b))
    a_last = send(a_near, Y_FAR)
    q_late, b = lax.optimization_barrier((q_own, b))
    q_other = send(q_late, CORE)

    q = jnp.stack([q_own, q_other])

    early = [a, a_near, a_far, b]
    state = attend_pieces(info, rows, zs, q, early, 0, state, skip_own=1)
    b_near, state = lax.optimization_barrier((b_near, state))
    b_last = send(b_near, Y_FAR)
    middle = [a_last, b_near]
    state = attend_pieces(info, rows, zs, q, middle, 4, state)
    pieces = early + middle + [b_far, b_last]
    keep, give = attend_last(info, rows, zs, q, state, pieces, 2)
    home = merge(keep, send(give, CORE))
    home, out_weight = lax.optimization_barrier((home, out_weight))
    w_far = load_columns(info, out_weight, 8)
    away = send(home, SWAP_BACK)

    far_give, far_keep = project(info, home, away, w_far)
    far = (far_keep + send(far_give, CORE).astype(jnp.float32)).astype(jnp.bfloat16)
    home, out_weight, far = lax.optimization_barrier((home, out_weight, far))
    far = send(far, XHI)
    near_give, near_keep = project(info, home, away, load_columns(info, out_weight, 7))
    near = near_keep + send(near_give, CORE).astype(jnp.float32)
    return (near + far.astype(jnp.float32)).astype(jnp.bfloat16)


def solution(mesh):
    in_specs = (
        P("seq", "head", None),
        P("seq", "head", None),
        P("seq", "head", None),
        P("head", None),
    )
    out_specs = P("seq", "head")
    return jax.shard_map(
        on_device, mesh=mesh, in_specs=in_specs, out_specs=out_specs, check_vma=False
    )
```

```python
import functools
import math

import jax
import jax.numpy as jnp
from jax import lax
from jax.experimental import pallas as pl
from jax.experimental.pallas import tpu as pltpu
from jax.sharding import PartitionSpec as P

NY, NX, NZ = 4, 2, 8
TOK = 256
HEADS = 8
HD = 128
ROWS = TOK * HEADS
DEEP = HD + 16
SLOTS = NY * NZ
KEYS = SLOTS * TOK
KT = 1024
RC = 512
PER_TILE = KT // TOK
SCALE2 = math.log2(math.e) / math.sqrt(HD)
LOW, HIGH = 1e-20, 1e34
NEG = -1e30
AXES = ("seq", "head")
BOTH = (((1,), (1,)), ((), ()))


def device(X, y, x, z, c):
    return ((y % NY) * 16 + x * 8 + z % NZ) * 4 + X * 2 + c


def perm_of(f):
    return [
        (device(X, y, x, z, c), device(*f(X, y, x, z, c)))
        for y in range(NY)
        for x in range(NX)
        for z in range(NZ)
        for X in range(2)
        for c in range(2)
    ]


def sign_of(pos, c):
    return 1 - 2 * ((pos + c) % 2)


SWAP = perm_of(lambda X, y, x, z, c: (X, y, x, z, c) if c == x else (X, 3 - y, 1 - x, z, 1 - c))
KV_SWAP = perm_of(lambda X, y, x, z, c: (X, y, x, z, c) if c == x else (X, y, 1 - x, z, 1 - c))
SWAP_BACK = [pair for pair in SWAP if pair[0] != pair[1]]
CORE = perm_of(lambda X, y, x, z, c: (X, y, x, z, 1 - c))
XHI = perm_of(lambda X, y, x, z, c: (1 - X, y, x, z, c))
Z_NEAR = perm_of(lambda X, y, x, z, c: (X, y, x, z + sign_of(z, c), c))
Z_FAR = perm_of(lambda X, y, x, z, c: (X, y, x, z - sign_of(z, c), c))
Z_SKIP = perm_of(lambda X, y, x, z, c: (X, y, x, z + 2 * sign_of(z, c), c))
Y_NEAR = perm_of(lambda X, y, x, z, c: (X, y + sign_of(y, c), x, z, c))
Y_FAR = perm_of(lambda X, y, x, z, c: (X, y - sign_of(y, c), x, z, c))


def send(value, perm):
    return lax.ppermute(value, AXES, perm)


def score(k, q):
    return lax.dot_general(k, q, BOTH, preferred_element_type=jnp.float32) * SCALE2


def mask_tile(s, aheads):
    key = lax.broadcasted_iota(jnp.int32, (TOK, RC), 0)
    tok = lax.broadcasted_iota(jnp.int32, (TOK, RC), 1) % TOK
    parts = []
    for i, ahead in enumerate(aheads):
        parts.append(jnp.where(key <= tok + ahead, s[i * TOK : (i + 1) * TOK, :], NEG))
    return jnp.concatenate(parts, axis=0)


def fast_tile(q_ref, k_ref, v_ref, acc, block, t, aheads):
    k, v = k_ref[t], v_ref[t]
    s = score(k, q_ref[block, :RC, :])
    for r in range(0, ROWS, RC):
        if aheads is not None:
            s = mask_tile(s, aheads)
        p = jnp.exp2(s).astype(jnp.bfloat16)
        if r + RC < ROWS:
            s = score(k, q_ref[block, r + RC : r + 2 * RC, :])
        acc[block, :, r : r + RC] += jnp.dot(v, p, preferred_element_type=jnp.float32)


def slow_tile(q_ref, k_ref, v_ref, acc, top, block, t, aheads):
    def chunk(r, _):
        at = pl.ds(pl.multiple_of(r * RC, RC), RC)
        s = mask_tile(score(k_ref[t], q_ref[block, at, :]), aheads)
        old = top[:1, at]
        new = jnp.maximum(old, jnp.max(s, axis=0, keepdims=True))
        p = jnp.exp2(s - new).astype(jnp.bfloat16)
        sums = jnp.dot(v_ref[t], p, preferred_element_type=jnp.float32)
        acc[block, :, at] = acc[block, :, at] * jnp.exp2(old - new) + sums
        top[:, at] = jnp.broadcast_to(new, (8, RC))
        return 0

    lax.fori_loop(0, ROWS // RC, chunk, 0)


def tiles(run, info, rows, zs, first, n_tiles, base, block, split, skip=0):
    def step(t, _):
        at = (first + t) * PER_TILE
        row = rows[first + t]
        nearest = zs[at]
        for i in range(1, PER_TILE):
            nearest = jnp.minimum(nearest, zs[at + i])
        whole = row < info[block]
        part = jnp.logical_and(row == info[2 + block], nearest <= info[4])
        aheads = [(info[4] - zs[at + i]) * TOK for i in range(PER_TILE)]
        if split:
            pl.when(whole)(lambda: run(base + t, None))
            pl.when(part)(lambda: run(base + t, aheads))
        else:
            aheads = [jnp.where(whole, TOK, ahead) for ahead in aheads]
            pl.when(jnp.logical_or(whole, part))(lambda: run(base + t, aheads))
        return 0

    lax.fori_loop(skip, n_tiles, step, 0)


def place(piece, k_ref, v_ref, t):
    for i in range(PER_TILE):
        src, dst = 2 * i * TOK, i * TOK
        k_ref[t, dst : dst + TOK, :] = piece[src : src + TOK, :]
        for j in range(0, TOK, HD):
            values = piece[src + TOK + j : src + TOK + j + HD, :]
            v_ref[t, :HD, dst + j : dst + j + HD] = values
    v_ref[t, HD:, :] = jnp.ones((DEEP - HD, KT), jnp.bfloat16)


def fast_blocks(info, rows, zs, first, n_tiles, base, q_ref, k_ref, v_ref, acc, skip_own=0):
    def block_step(block, _):
        def run(t, aheads):
            fast_tile(q_ref, k_ref, v_ref, acc, block, t, aheads)

        skip = jnp.where(block == 0, skip_own, 0)
        tiles(run, info, rows, zs, first, n_tiles, base, block, True, skip)
        return 0

    lax.fori_loop(0, q_ref.shape[0], block_step, 0)


def piece_kernel(first, n_tiles, has_state, skip_own, info, rows, zs, q_ref, *refs):
    pieces, refs = refs[:n_tiles], refs[n_tiles:]
    acc, k_ref, v_ref = refs[-3:]
    if not has_state:
        acc[...] = jnp.zeros_like(acc)
    for t, piece in enumerate(pieces):
        place(piece, k_ref, v_ref, t)
    fast_blocks(info, rows, zs, first, n_tiles, 0, q_ref, k_ref, v_ref, acc, skip_own)


def tile_scratch(n):
    return [pltpu.VMEM((n, KT, HD), jnp.bfloat16), pltpu.VMEM((n, DEEP, KT), jnp.bfloat16)]


VMEM = pl.BlockSpec(memory_space=pltpu.VMEM)
SMEM = pl.BlockSpec(memory_space=pltpu.SMEM)
STATE = jax.ShapeDtypeStruct((2, DEEP, ROWS), jnp.float32)
PART = jax.ShapeDtypeStruct((DEEP, ROWS), jnp.float32)
GIVEN = jax.ShapeDtypeStruct((DEEP, ROWS), jnp.bfloat16)


def cost(n_tiles):
    return pl.CostEstimate(
        flops=8 * n_tiles * ROWS * KT * HD,
        bytes_accessed=4 * 2**20,
        transcendentals=n_tiles * ROWS * KT,
    )


def attend_pieces(info, rows, zs, q, pieces, first, state=None, skip_own=0):
    n_tiles = len(pieces)
    extra = [] if state is None else [state]
    return pl.pallas_call(
        functools.partial(piece_kernel, first, n_tiles, state is not None, skip_own),
        out_shape=STATE,
        in_specs=[SMEM, SMEM, SMEM, VMEM] + [VMEM] * (n_tiles + len(extra)),
        out_specs=VMEM,
        scratch_shapes=tile_scratch(n_tiles),
        compiler_params=pltpu.CompilerParams(vmem_limit_bytes=20 * 2**20),
        input_output_aliases={} if state is None else {4 + n_tiles: 0},
        cost_estimate=cost(n_tiles),
        name=f"attend_{first}_{n_tiles}",
    )(info, rows, zs, q, *pieces, *extra)


def in_parts(row, n):
    parts = []
    for _ in range(n):
        parts.append(row.astype(jnp.bfloat16).astype(jnp.float32))
        row = row - parts[-1]
    return parts


def last_kernel(n_pieces, info, rows, zs, q_ref, state, *refs):
    pieces = refs[:n_pieces]
    acc, keep_ref, give_ref, k_ref, v_ref, top = refs[n_pieces:]
    last = n_pieces - 1
    place(pieces[last], k_ref, v_ref, last)
    fast_blocks(info, rows, zs, last, 1, last, q_ref, k_ref, v_ref, acc)
    for block in range(2):
        total = acc[block, HD : HD + 8, :]
        bad = jnp.logical_not(jnp.logical_and(total >= LOW, total <= HIGH))
        n_bad = jnp.sum(jnp.max(bad.astype(jnp.float32), axis=0, keepdims=True))
        some = jnp.logical_or(info[block] > 0, info[2 + block] >= 0)
        top[...] = jnp.full((8, ROWS), jnp.where(some, 0.0, NEG), jnp.float32)

        @pl.when(jnp.logical_and(some, n_bad > 0.0))
        def _(block=block):
            acc[block] = jnp.zeros((DEEP, ROWS), jnp.float32)
            top[...] = jnp.full((8, ROWS), NEG, jnp.float32)
            for t, piece in enumerate(pieces[:last]):
                place(piece, k_ref, v_ref, t)

            def run(t, aheads):
                slow_tile(q_ref, k_ref, v_ref, acc, top, block, t, aheads)

            tiles(run, info, rows, zs, 0, n_pieces, 0, block, False)

        if block == 0:
            keep_ref[: HD + 8, :] = acc[block, : HD + 8, :]
            keep_ref[HD + 8 :, :] = top[...]
        else:
            give_ref[:HD, :] = acc[block, :HD, :].astype(jnp.bfloat16)
            parts = in_parts(acc[block, HD : HD + 1, :], 2) + in_parts(top[:1, :], 3)
            row = lax.broadcasted_iota(jnp.int32, (DEEP - HD, ROWS), 0)
            ends = jnp.zeros((DEEP - HD, ROWS), jnp.float32)
            for i, part in enumerate(parts):
                ends = jnp.where(row == i, part, ends)
            give_ref[HD:, :] = ends.astype(jnp.bfloat16)


def attend_last(info, rows, zs, q, state, pieces):
    return pl.pallas_call(
        functools.partial(last_kernel, len(pieces)),
        out_shape=(STATE, PART, GIVEN),
        in_specs=[SMEM, SMEM, SMEM] + [VMEM] * (2 + len(pieces)),
        out_specs=(VMEM, VMEM, VMEM),
        scratch_shapes=tile_scratch(len(pieces)) + [pltpu.VMEM((8, ROWS), jnp.float32)],
        input_output_aliases={4: 0},
        compiler_params=pltpu.CompilerParams(vmem_limit_bytes=20 * 2**20),
        cost_estimate=cost(1),
        name="attend_last",
    )(info, rows, zs, q, state, *pieces)[1:]


def merge_kernel(a_ref, b_ref, out_ref):
    a_sum, a_top = a_ref[HD : HD + 1, :], a_ref[HD + 8 : HD + 9, :]
    ends = b_ref[HD:, :].astype(jnp.float32)
    b_sum = ends[0:1] + ends[1:2]
    b_top = ends[2:3] + ends[3:4] + ends[4:5]
    top = jnp.maximum(a_top, b_top)
    fa, fb = jnp.exp2(a_top - top), jnp.exp2(b_top - top)
    total = a_sum * fa + b_sum * fb
    fa, fb = fa / total, fb / total
    for h in range(HEADS):
        at = slice(h * TOK, (h + 1) * TOK)
        value = a_ref[:HD, at] * fa[:, at] + b_ref[:HD, at].astype(jnp.float32) * fb[:, at]
        out_ref[:, h * HD : (h + 1) * HD] = value.T.astype(jnp.bfloat16)


def merge(a, b):
    return pl.pallas_call(
        merge_kernel,
        out_shape=jax.ShapeDtypeStruct((TOK, HEADS * HD), jnp.bfloat16),
        in_specs=[VMEM, VMEM],
        out_specs=VMEM,
        compiler_params=pltpu.CompilerParams(vmem_limit_bytes=8 * 2**20),
        name="merge",
    )(a, b)


def pack_kernel(k_ref, v_ref, out_ref):
    out_ref[:TOK, :] = k_ref[...]
    for j in range(0, TOK, HD):
        out_ref[TOK + j : TOK + j + HD, :] = v_ref[j : j + HD, :].T


def pack(k, v):
    return pl.pallas_call(
        pack_kernel, out_shape=jax.ShapeDtypeStruct((2 * TOK, HD), jnp.bfloat16), name="pack"
    )(k, v)


COLS = 512
SLICE = 1024


def load_kernel(first, info, w_ref, out_ref, sem):
    col = pl.multiple_of(info[first] * SLICE, SLICE)
    copy = pltpu.make_async_copy(w_ref.at[:, pl.ds(col, 2 * SLICE)], out_ref, sem)
    copy.start()
    copy.wait()


def load_columns(info, w, first):
    return pl.pallas_call(
        functools.partial(load_kernel, first),
        out_shape=jax.ShapeDtypeStruct((w.shape[0], 2 * SLICE), w.dtype),
        in_specs=[SMEM, pl.BlockSpec(memory_space=pltpu.HBM)],
        out_specs=VMEM,
        scratch_shapes=[pltpu.SemaphoreType.DMA],
        compiler_params=pltpu.CompilerParams(vmem_limit_bytes=4 * 2**20),
        cost_estimate=pl.CostEstimate(flops=0, bytes_accessed=2**23, transcendentals=0),
        name=f"load_{first}",
    )(info, w)


def project_kernel(info, home_ref, away_ref, w_ref, give_ref, keep_ref, x_ref):
    x_ref[...] = home_ref[...]

    @pl.when(info[5] == 0)
    def _():
        x_ref[...] = away_ref[...]

    for out_ref, side in ((give_ref, 1 - info[6]), (keep_ref, info[6])):
        for j in range(0, SLICE, COLS):
            at = pl.ds(pl.multiple_of(side * SLICE + j, COLS), COLS)
            value = jnp.dot(x_ref[...], w_ref[:, at], preferred_element_type=jnp.float32)
            out_ref[:, j : j + COLS] = value.astype(out_ref.dtype)


def project(info, home, away, w):
    return pl.pallas_call(
        project_kernel,
        out_shape=(
            jax.ShapeDtypeStruct((TOK, SLICE), jnp.bfloat16),
            jax.ShapeDtypeStruct((TOK, SLICE), jnp.float32),
        ),
        in_specs=[SMEM, VMEM, VMEM, VMEM],
        out_specs=(VMEM, VMEM),
        scratch_shapes=[pltpu.VMEM((TOK, SLICE), jnp.bfloat16)],
        compiler_params=pltpu.CompilerParams(vmem_limit_bytes=8 * 2**20),
        name="project",
    )(info, home, away, w)


def on_device(queries, key_states, value_vectors_all, out_weight):
    seq = lax.axis_index("seq")
    head = lax.axis_index("head")
    y, x, z = seq // 16, (seq // 8) % 2, seq % 8
    X, c = head // 2, head % 2
    diagonal = c == x

    k = key_states.reshape(TOK, HD)
    v = value_vectors_all.reshape(TOK, HD)
    kv = send(pack(k, v), KV_SWAP)
    q = queries.transpose(1, 0, 2).reshape(ROWS, HD)
    kv, q = lax.optimization_barrier((kv, q))

    sz, sy = sign_of(z, c), sign_of(y, c)
    near_z, far_z, skip_z = send(kv, Z_NEAR), send(kv, Z_FAR), send(kv, Z_SKIP)
    q_own = send(q, SWAP)
    near_z, far_z, skip_z, q_own = lax.optimization_barrier((near_z, far_z, skip_z, q_own))
    side = jnp.concatenate([far_z, skip_z], axis=0)
    a = jnp.concatenate([kv, near_z, side], axis=0)
    a_near, a_far = send(a, Y_NEAR), send(a, Y_FAR)
    own_row = jnp.where(diagonal, y, NY - 1 - y)
    other_rows = NY - 1 - own_row + jnp.where(c == 0, 1, 0)
    info = jnp.stack([own_row, other_rows, own_row, jnp.int32(-1), z, diagonal, c, 2 * X, 2 - 2 * X]).astype(jnp.int32)
    near, far, last = y + sy, y - sy, y - 2 * sy
    rows = jnp.stack([w % NY for w in (y, near, far, y, last, near, far, last)]).astype(jnp.int32)
    z_a = [z, z + sz, z - sz, z - 2 * sz]
    z_b = [z + 2 * sz, z + 3 * sz, z - 3 * sz, z - 4 * sz]
    zs = jnp.stack([w % NZ for w in z_a * 3 + z_b + z_a + z_b * 3]).astype(jnp.int32)
    state = attend_pieces(info, rows, zs, q_own[None], [a], 0)
    b_1, b_2 = send(side, Z_NEAR), send(side, Z_SKIP)
    b_1, b_2, state = lax.optimization_barrier((b_1, b_2, state))
    b = jnp.concatenate([b_1, b_2], axis=0)
    b_near, b_far = send(b, Y_NEAR), send(b, Y_FAR)
    a_near, a_far, b = lax.optimization_barrier((a_near, a_far, b))
    a_last = send(a_near, Y_FAR)
    q_late, b = lax.optimization_barrier((q_own, b))
    q_other = send(q_late, CORE)

    q = jnp.stack([q_own, q_other])

    early = [a, a_near, a_far, b]
    state = attend_pieces(info, rows, zs, q, early, 0, state, skip_own=1)
    b_near, state = lax.optimization_barrier((b_near, state))
    b_last = send(b_near, Y_FAR)
    middle = [a_last, b_near, b_far]
    state = attend_pieces(info, rows, zs, q, middle, 4, state)
    pieces = early + middle + [b_last]
    keep, give = attend_last(info, rows, zs, q, state, pieces)
    home = merge(keep, send(give, CORE))
    home, out_weight = lax.optimization_barrier((home, out_weight))
    w_far = load_columns(info, out_weight, 8)
    away = send(home, SWAP_BACK)

    far_give, far_keep = project(info, home, away, w_far)
    far = (far_keep + send(far_give, CORE).astype(jnp.float32)).astype(jnp.bfloat16)
    home, out_weight, far = lax.optimization_barrier((home, out_weight, far))
    far = send(far, XHI)
    near_give, near_keep = project(info, home, away, load_columns(info, out_weight, 7))
    near = near_keep + send(near_give, CORE).astype(jnp.float32)
    return (near + far.astype(jnp.float32)).astype(jnp.bfloat16)


def solution(mesh):
    in_specs = (
        P("seq", "head", None),
        P("seq", "head", None),
        P("seq", "head", None),
        P("head", None),
    )
    out_specs = P("seq", "head")
    return jax.shard_map(
        on_device, mesh=mesh, in_specs=in_specs, out_specs=out_specs, check_vma=False
    )
```
